128 devices in a mesh: tm: 16 (over z, x), dish: 8 (over y, core).
Axes of the slice: x: 4, y: 4, z: 4, core: 2. Of those that a mesh axis runs over, the one named last changes fastest.
Arguments:
- tod: float32 [64, 1024, 4096], P('dish', None, 'tm'), may hold values from -8 to 8
- taps: float32 [65], replicated, may hold values from 0.005 to 0.025
- modes_init: float32 [6, 1024], replicated, may hold values from -6 to 6
- weights: float32 [64, 4096], P('dish', 'tm'), may hold values from 0.25 to 4
- block_tile: int32 [64, 32], P('dish', 'tm'), may hold values from 0 to 15, as said below
- block_offset: int32 [64, 32], P('dish', 'tm'), may hold values from 0 to 255
Outputs:
- sky: float32 [16, 1024, 256], P('tm', 'dish')
The draws below stay inside these ranges and needn't reach their ends.
Inputs may be any that keep to these rules, and one draw needn't show every extreme that they name: `block_tile`: among the blocks of one device (its 8 dishes and its 2 blocks of time), no tile is named more than 2 times, and one tile is named exactly 2 times by the blocks of every device.
All inputs are finite; a program needn't handle non-finite values.
Results may differ from the reference program's by a relative error of at most 0.002.
The reference program's roundings to bfloat16 on the way (of `weighted`) count: a program that leaves them out, or rounds other values in their place, can miss the bound.
Values may be sent and summed in bfloat16 or wider, within the bound.
No kernel may reach another device: no remote copies, remote signals or barrier semaphores. Data moves between devices by JAX's collectives and lax.ppermute only.
A program may use at most 128 MiB of HBM per device.

```python
import math
import jax
import jax.numpy as jnp
from jax import lax

CH = 1024
DISH_DEV = 8
TDEV = 256
TAPS = 65
MODES = 6
ITERS = 3
BLOCK = 128
PIX = 256
DISH = 64
SAMPLES = 4096
NBLKS = 32
TILES = 16
N_TM = 16
N_DISH = 8


def draw_block_tile(key, part):
    key = jax.random.fold_in(key, 7)
    blocks_dev = DISH_DEV * (TDEV // BLOCK)
    most = max(2, (2 * blocks_dev + N_TM - 1) // N_TM)
    hottest = jax.random.randint(jax.random.fold_in(key, 1), (), 0, N_TM)
    device_keys = jax.random.split(jax.random.fold_in(key, 2), N_TM * N_DISH)

    def one_device(device_key):
        first_key, second_key = jax.random.split(device_key)
        others = (jnp.arange((N_TM - 1) * most) // most + hottest + 1) % N_TM
        chosen = others[jax.random.permutation(first_key, (N_TM - 1) * most)[:blocks_dev - most]]
        owners = jnp.concatenate([jnp.full((most,), hottest, jnp.int32), chosen.astype(jnp.int32)])
        return owners[jax.random.permutation(second_key, blocks_dev)]
    table = jax.vmap(one_device)(device_keys).reshape(N_TM, N_DISH, DISH_DEV, TDEV // BLOCK)
    return table.transpose(1, 2, 0, 3).reshape(DISH, NBLKS).astype(jnp.int32)


def set_ends(drawn, stream_key, least, high):
    longest = drawn.shape.index(max(drawn.shape))
    spots = []
    for shift in (0, 1):
        where = [jax.random.randint(jax.random.fold_in(stream_key, axis), (), 0, length) for axis, length in enumerate(drawn.shape)]
        where[longest] = (where[longest] + shift) % drawn.shape[longest]
        spots.append(tuple(where))
    return drawn.at[spots[0]].set(least).at[spots[1]].set(high)


def steps_of(stream_key, extent, cuts, low, top_value):
    loudness, own = 1.0, jax.random.fold_in(stream_key, 6)
    for position, parts in cuts:
        steps = jnp.exp(jax.random.uniform(jax.random.fold_in(own, position), (parts,), jnp.float32, low / len(cuts), top_value / len(cuts)))
        loudness = loudness * jnp.repeat(steps, extent[position] // parts).reshape([-1 if axis == position else 1 for axis in range(len(extent))])
    return loudness


def scatter_about(stream_key, extent, scale, bound, cuts=(), kind=jnp.bfloat16):
    loudness = steps_of(stream_key, extent, cuts, -0.22, 0.18) if cuts else 1.0
    array = jax.random.normal(stream_key, extent, jnp.float32) * scale * loudness
    return jnp.minimum(jnp.maximum(array, -bound), bound).astype(kind)


def setup_inputs(seed: int = 0) -> dict:
    key_of = jax.random.split(jax.random.key(seed), 7)
    return {
        "tod": scatter_about(key_of[0], (DISH, CH, SAMPLES), 1.0, 8.0, ((0, 8), (2, 16)), jnp.float32),
        "taps": jnp.clip(jax.random.uniform(key_of[1], (TAPS,), jnp.float32, 0.005, 0.025), 0.005, 0.025),
        "modes_init": scatter_about(key_of[2], (MODES, CH), 1.0, 6.0, (), jnp.float32),
        "weights": jnp.clip(jnp.exp(math.log(4.0) - 2.7725887 * jax.random.uniform(key_of[3], (DISH, SAMPLES), jnp.float32) ** steps_of(key_of[3], (DISH, SAMPLES), ((0, 8), (1, 16)), -0.2, 0.2)), 0.25, 4.0),
        "block_tile": draw_block_tile(jax.random.fold_in(key_of[6], 71), 0),
        "block_offset": set_ends(jax.random.randint(key_of[5], (DISH, NBLKS), 0, PIX), jax.random.fold_in(key_of[5], 1), 0, PIX - 1).astype(jnp.int32),
    }


def orth(rows):
    result = []
    for index in range(rows.shape[0]):
        vector = rows[index]
        for done in result:
            vector = vector - jnp.sum(vector * done) * done
        result.append(vector / jnp.sqrt(jnp.sum(vector * vector)))
    return jnp.stack(result)

def reference(tod, taps, modes_init, weights, block_tile, block_offset):
    reach = (TAPS - 1) // 2
    length = tod.shape[2]

    def highpass(series):
        padded = jnp.pad(series, ((0, 0), (reach, reach)))
        lowpass = jnp.zeros_like(series)
        for index in range(TAPS):
            lowpass = lowpass + taps[index] * padded[:, index:index + length]
        return series - lowpass
    filtered = lax.map(highpass, tod)

    def add_cov(total, series):
        return (total + jnp.dot(series, series.T, precision=lax.Precision.HIGHEST), None)
    cov, unused = lax.scan(add_cov, jnp.zeros((CH, CH), jnp.float32), filtered)
    basis = orth(modes_init)
    for step in range(ITERS):
        basis = orth(jnp.dot(basis, cov, precision=lax.Precision.HIGHEST))
    within = jnp.arange(BLOCK, dtype=jnp.int32)

    def add_dish(sky_flat, inputs):
        series, weight_row, tiles_row, offset_row = inputs
        amounts = jnp.dot(basis, series, precision=lax.Precision.HIGHEST)
        cleaned = series - jnp.dot(basis.T, amounts, precision=lax.Precision.HIGHEST)
        weighted = (weight_row[None, :] * cleaned).astype(jnp.bfloat16).astype(jnp.float32)
        column = tiles_row[:, None] * PIX + (offset_row[:, None] + within[None, :]) % PIX
        column = column.reshape(-1).astype(jnp.int32)
        return (sky_flat.at[:, column].add(weighted), None)
    sky_flat, unused = lax.scan(add_dish, jnp.zeros((CH, TILES * PIX), jnp.float32), (filtered, weights, block_tile, block_offset))
    return sky_flat.reshape(CH, TILES, PIX).transpose(1, 0, 2)
```

```python
import jax
import jax.numpy as jnp
from jax import lax
from jax.experimental import pallas as pl
from jax.experimental.pallas import tpu as pltpu
from jax.sharding import Mesh
from jax.sharding import PartitionSpec as P

ITERS = 3
BLOCK = 128
PIX = 256
MODES = 6
ROWS = 8
CHIPS = 4
CORES = 2
F32 = jnp.float32
BF16 = jnp.bfloat16
PARAMS = pltpu.CompilerParams(vmem_limit_bytes=24 * 1024 * 1024)
VMEM = pl.BlockSpec(memory_space=pltpu.VMEM)
SMEM = pl.BlockSpec(memory_space=pltpu.SMEM)
LAST = (((1,), (1,)), ((), ()))


def split(value, pieces):
    result = []
    for _ in range(pieces):
        piece = value.astype(BF16)
        result.append(piece)
        value = value - piece.astype(F32)
    return result


def rows_of(pieces):
    return jnp.concatenate([piece.astype(F32) for piece in pieces], axis=0).astype(BF16)


def folded(product, pieces):
    total = product[0:ROWS]
    for index in range(1, pieces):
        total = total + product[index * ROWS:(index + 1) * ROWS]
    return total


def mxu(left, right):
    return jnp.dot(left, right, preferred_element_type=F32)


def mxu_last(left, right):
    return lax.dot_general(left, right, LAST, preferred_element_type=F32)


def orth(rows):
    row = lax.broadcasted_iota(jnp.int32, rows.shape, 0)
    for index in range(MODES):
        vector = rows[index:index + 1]
        inner = jnp.sum(rows * vector, axis=1, keepdims=True)
        square = inner[index:index + 1]
        later = rows - (inner / square) * vector
        unit = vector / jnp.sqrt(square)
        rows = jnp.where(row == index, unit, jnp.where(row > index, later, rows))
    return jnp.where(row < MODES, rows, 0.0)


def pack_kernel(reach, tod_ref, head_ref, tail_ref):
    groups = BLOCK // reach
    dishes, chans, tdev = tod_ref.shape
    size = chans // groups
    lane = lax.broadcasted_iota(jnp.int32, (size, BLOCK), 1) // reach

    def body(dish, carry):
        head = jnp.zeros((size, BLOCK), F32)
        tail = jnp.zeros((size, BLOCK), F32)
        for group in range(groups):
            rows = pl.ds(group * size, size)
            first = tod_ref[dish, rows, 0:BLOCK]
            last = tod_ref[dish, rows, tdev - BLOCK:tdev]
            if group:
                first = pltpu.roll(first, group * reach, 1)
            move = (group * reach + reach) % BLOCK
            if move:
                last = pltpu.roll(last, move, 1)
            head = jnp.where(lane == group, first, head)
            tail = jnp.where(lane == group, last, tail)
        head_ref[dish] = head
        tail_ref[dish] = tail
        return carry

    lax.fori_loop(0, dishes, body, 0)


def taps_at(taps_ref, lag):
    def body(index, band):
        return jnp.where(lag == index, taps_ref[index], band)

    return lax.fori_loop(0, taps_ref.shape[0], body, jnp.zeros(lag.shape, F32), unroll=5)


def own_kernel(reach, taps_ref, modes_ref, tod_ref, basis_ref, fix_ref, own_ref, band):
    dishes, chans, tdev = tod_ref.shape
    groups = BLOCK // reach
    part = 64
    source = lax.broadcasted_iota(jnp.int32, (part, tdev), 0)
    target = lax.broadcasted_iota(jnp.int32, (part, tdev), 1)
    for start in range(0, tdev, part):
        pieces = split(taps_at(taps_ref, source + (start + reach) - target), 2)
        band[0, start:start + part] = pieces[0]
        band[1, start:start + part] = pieces[1]
    source = lax.broadcasted_iota(jnp.int32, (reach, tdev), 0)
    target = lax.broadcasted_iota(jnp.int32, (reach, tdev), 1)
    fix_ref[...] = jnp.zeros_like(fix_ref)
    for side, shift in ((0, 0), (1, tdev + reach)):
        pieces = split(taps_at(taps_ref, source + shift - target), 2)
        for group in range(groups):
            rows = pl.ds(side * BLOCK + group * reach, reach)
            fix_ref[0, group, rows, :] = pieces[0]
            fix_ref[1, group, rows, :] = pieces[1]
    basis_ref[...] = orth(modes_ref[...])
    size = 256

    def body(dish, carry):
        for start in range(0, chans, size):
            rows = pl.ds(start, size)
            series = tod_ref[dish, rows, :]
            high, low = split(series, 2)
            lowpass = mxu(high, band[0]) + (mxu(high, band[1]) + mxu(low, band[0]))
            own_ref[dish, rows, :] = series - lowpass
        return carry

    lax.fori_loop(0, dishes, body, 0)


def step(basis, high_ref, mid_ref):
    dishes, chans = high_ref.shape[0], high_ref.shape[1]
    left = rows_of(split(basis, 2))
    amounts = []
    for dish in range(dishes):
        product = folded(mxu(left, high_ref[dish]) + mxu(left, mid_ref[dish]), 2)
        amounts.append(rows_of(split(product, 2)))
    total = jnp.zeros((2 * ROWS, chans), F32)
    for dish in range(dishes):
        total = total + (
            mxu_last(amounts[dish], high_ref[dish]) + mxu_last(amounts[dish], mid_ref[dish])
        )
    return folded(total, 2)


def edge_kernel(basis_ref, fix_ref, own_ref, left_ref, right_ref, pointing_ref,
                high_ref, mid_ref, low_ref, total_ref):
    dishes, chans = own_ref.shape[0], own_ref.shape[1]
    groups = fix_ref.shape[1]
    size = chans // groups

    def body(dish, carry):
        edges = jnp.concatenate([left_ref[dish], right_ref[dish]], axis=1)
        high, low = split(edges, 2)
        for group in range(groups):
            rows = pl.ds(group * size, size)
            lowpass = mxu(high, fix_ref[0, group]) + (
                mxu(high, fix_ref[1, group]) + mxu(low, fix_ref[0, group])
            )
            pieces = split(own_ref[dish, rows, :] - lowpass, 3)
            high_ref[dish, rows, :] = pieces[0]
            mid_ref[dish, rows, :] = pieces[1]
            low_ref[dish, rows, :] = pieces[2]
        return carry

    lax.fori_loop(0, dishes, body, 0)
    total_ref[...] = step(basis_ref[...], high_ref, mid_ref)
    total_ref[MODES:MODES + 1] = pointing_ref[...]


def step_kernel(sums_ref, high_ref, mid_ref, total_ref):
    total_ref[...] = step(orth(sums_ref[...]), high_ref, mid_ref)


def clean_kernel(sums_ref, weight_ref, high_ref, mid_ref, low_ref, out_ref):
    dishes, chans, tdev = high_ref.shape
    basis = split(orth(sums_ref[...]), 3)
    left = rows_of(basis)
    spread = rows_of([basis[i] for i in (0, 0, 0, 1, 1, 2)])
    per_dish = tdev // BLOCK
    owned = chans // (CHIPS * CORES)
    part = owned // CHIPS

    def body(dish, carry):
        product = mxu(left, low_ref[dish]) + mxu(left, mid_ref[dish]) + mxu(left, high_ref[dish])
        amounts = split(folded(product, 3), 3)
        right = rows_of([amounts[i] for i in (0, 1, 2, 0, 1, 0)])
        weight = weight_ref[dish]
        for group in range(CHIPS * CORES):
            rows = pl.ds(group * owned, owned)
            filtered = (low_ref[dish, rows, :].astype(F32) + mid_ref[dish, rows, :].astype(F32)
                        ) + high_ref[dish, rows, :].astype(F32)
            removed = lax.dot_general(
                spread[:, group * owned:(group + 1) * owned], right,
                (((0,), (0,)), ((), ())), preferred_element_type=F32,
            )
            weighted = (weight * (filtered - removed)).astype(BF16)
            for chip in range(CHIPS):
                for block in range(per_dish):
                    out_ref[chip * CHIPS * CORES + group, dish * per_dish + block] = weighted[
                        chip * part:(chip + 1) * part, block * BLOCK:(block + 1) * BLOCK
                    ]
        return carry

    lax.fori_loop(0, dishes, body, 0)


def bin_kernel(pointing_ref, blocks_ref, sky_ref):
    sky_ref[...] = jnp.zeros_like(sky_ref)
    sources, count, chans, width = blocks_ref.shape
    lane = lax.broadcasted_iota(jnp.int32, (chans, width), 1)

    def body(source, carry):
        for block in range(count):
            where = source * 2 * count + block
            tile = pointing_ref[where]
            offset = pointing_ref[where + count]
            half = offset // width
            shift = offset - half * width
            moved = pltpu.roll(blocks_ref[source, block].astype(F32), shift, 1)
            first = jnp.where((lane >= shift) == (half == 0), moved, 0.0)
            sky_ref[tile, :, 0:width] += first
            sky_ref[tile, :, width:2 * width] += moved - first
        return carry

    lax.fori_loop(0, sources, body, 0)


def call(kernel, name, out_shape, in_specs, scratch=()):
    several = isinstance(out_shape, (list, tuple))
    return pl.pallas_call(
        kernel,
        out_shape=out_shape,
        in_specs=in_specs,
        out_specs=[VMEM] * len(out_shape) if several else VMEM,
        scratch_shapes=scratch,
        compiler_params=PARAMS,
        name=name,
    )


def total_over(value, axes):
    for axis in axes:
        count = lax.axis_size(axis)
        parts = [value] + [
            lax.ppermute(value, axis, [(i, (i + s) % count) for i in range(count)])
            for s in range(1, count)
        ]
        while len(parts) > 1:
            parts = [a + b for a, b in zip(parts[::2], parts[1::2])]
        value = parts[0]
    return value


def shards(tod, taps, modes_init, weights, block_tile, block_offset):
    dishes, chans, tdev = tod.shape
    reach = (taps.shape[0] - 1) // 2
    groups = BLOCK // reach
    size = chans // groups
    per_dish = tdev // BLOCK
    times = CHIPS * CHIPS
    sharers = CHIPS * CHIPS * CORES
    part = chans // sharers
    rows_f32 = jax.ShapeDtypeStruct((ROWS, chans), F32)
    edge_f32 = jax.ShapeDtypeStruct((dishes, size, BLOCK), F32)
    piece = pltpu.VMEM((dishes, chans, tdev), BF16)

    with jax.named_scope("edges"):
        head, tail = call(
            lambda *refs: pack_kernel(reach, *refs), "pack", [edge_f32] * 2, [VMEM]
        )(tod)
        ends = times - 1
        from_left = lax.ppermute(tail, ("z", "x"), [(i, i + 1) for i in range(ends)])
        from_right = lax.ppermute(head, ("z", "x"), [(i + 1, i) for i in range(ends)])

    with jax.named_scope("own"):
        modes = jnp.pad(modes_init, ((0, ROWS - MODES), (0, 0)))
        basis, fix, own = call(
            lambda *refs: own_kernel(reach, *refs), "own",
            [rows_f32, jax.ShapeDtypeStruct((2, groups, tdev, tdev), BF16),
             pltpu.VMEM((dishes, chans, tdev), F32)],
            [SMEM, VMEM, VMEM],
            [pltpu.VMEM((2, tdev, tdev), BF16)],
        )(taps, modes, tod)

    with jax.named_scope("pointing"):
        mine = jnp.concatenate([block_tile.reshape(-1), block_offset.reshape(-1)]).astype(F32)
        slot = jnp.arange(sharers, dtype=jnp.int32)[:, None] == lax.axis_index(("x", "y", "c"))
        pointing = jnp.where(slot, mine[None, :], 0.0).reshape(1, sharers * mine.shape[0])

    with jax.named_scope("filtered"):
        high, mid, low, sums = call(
            edge_kernel, "edge", [piece, piece, piece, rows_f32], [VMEM] * 6
        )(basis, fix, own, from_left, from_right, pointing)

    with jax.named_scope("iterations"):
        sums = total_over(sums, ("c", "y", "x"))
        pointing = sums[MODES].astype(jnp.int32)
        sums = total_over(sums, ("z",))
        for _ in range(ITERS - 1):
            sums = call(step_kernel, "step", rows_f32, [VMEM] * 3)(sums, high, mid)
            sums = total_over(sums, ("c", "y", "x", "z"))

    with jax.named_scope("cleaned"):
        blocks = call(
            clean_kernel, "clean",
            jax.ShapeDtypeStruct((sharers, dishes * per_dish, part, BLOCK), BF16), [VMEM] * 5,
        )(sums, weights.reshape(dishes, 1, tdev), high, mid, low)

    with jax.named_scope("channels"):
        arrived = lax.all_to_all(blocks, ("x", "y", "c"), 0, 0, tiled=True)

    with jax.named_scope("binning"):
        sky = call(
            bin_kernel, "bin", jax.ShapeDtypeStruct((times, part, PIX), F32), [SMEM, VMEM]
        )(pointing, arrived)

    with jax.named_scope("tiles"):
        parts = lax.all_to_all(sky, ("z", "x"), 0, 0, tiled=True)
        parts = parts.reshape(CHIPS, CHIPS * part, PIX)
        return jnp.sum(parts, axis=0, keepdims=True)


def solution(mesh):
    chips = Mesh(mesh.devices.reshape(CHIPS, CHIPS, CHIPS, CORES), ("z", "x", "y", "c"))
    dish, time = ("y", "c"), ("z", "x")
    placed = (P(dish, None, time), P(), P(), P(dish, time), P(dish, time), P(dish, time))
    return jax.shard_map(
        shards, mesh=chips, in_specs=placed, out_specs=P(time, dish, None), check_vma=False
    )
```

```python
import jax
import jax.numpy as jnp
from jax import lax
from jax.experimental import pallas as pl
from jax.experimental.pallas import tpu as pltpu
from jax.sharding import Mesh
from jax.sharding import PartitionSpec as P

ITERS = 3
BLOCK = 128
PIX = 256
MODES = 6
ROWS = 8
CHIPS = 4
CORES = 2
F32 = jnp.float32
BF16 = jnp.bfloat16
PARAMS = pltpu.CompilerParams(vmem_limit_bytes=16 * 1024 * 1024)
VMEM = pl.BlockSpec(memory_space=pltpu.VMEM)
SMEM = pl.BlockSpec(memory_space=pltpu.SMEM)
LAST = (((1,), (1,)), ((), ()))


def split(value, pieces):
    result = []
    for _ in range(pieces):
        piece = value.astype(BF16)
        result.append(piece)
        value = value - piece.astype(F32)
    return result


def rows_of(pieces):
    return jnp.concatenate([piece.astype(F32) for piece in pieces], axis=0).astype(BF16)


def folded(product, pieces):
    total = product[0:ROWS]
    for index in range(1, pieces):
        total = total + product[index * ROWS:(index + 1) * ROWS]
    return total


def mxu(left, right):
    return jnp.dot(left, right, preferred_element_type=F32)


def mxu_last(left, right):
    return lax.dot_general(left, right, LAST, preferred_element_type=F32)


def orth(rows):
    row = lax.broadcasted_iota(jnp.int32, (rows.shape[0], 1), 0)
    squares = jnp.ones((rows.shape[0], 1), F32)
    for index in range(MODES):
        vector = rows[index:index + 1]
        inner = jnp.sum(rows * vector, axis=1, keepdims=True)
        square = inner[index:index + 1]
        squares = jnp.where(row == index, square, squares)
        rows = rows - jnp.where(row > index, inner / square, 0.0) * vector
    return jnp.where(row < MODES, rows / jnp.sqrt(squares), 0.0)


def pack_kernel(reach, tod_ref, head_ref, tail_ref):
    groups = BLOCK // reach
    dishes, chans, tdev = tod_ref.shape
    size = chans // groups
    lane = lax.broadcasted_iota(jnp.int32, (size, BLOCK), 1) // reach

    def body(dish, carry):
        head = jnp.zeros((size, BLOCK), F32)
        tail = jnp.zeros((size, BLOCK), F32)
        for group in range(groups):
            rows = pl.ds(group * size, size)
            first = tod_ref[dish, rows, 0:BLOCK]
            last = tod_ref[dish, rows, tdev - BLOCK:tdev]
            if group:
                first = pltpu.roll(first, group * reach, 1)
            move = (group * reach + reach) % BLOCK
            if move:
                last = pltpu.roll(last, move, 1)
            head = jnp.where(lane == group, first, head)
            tail = jnp.where(lane == group, last, tail)
        head_ref[dish] = head
        tail_ref[dish] = tail
        return carry

    lax.fori_loop(0, dishes, body, 0)


def taps_at(taps_ref, lag):
    def body(index, band):
        return jnp.where(lag == index, taps_ref[index], band)

    return lax.fori_loop(0, taps_ref.shape[0], body, jnp.zeros(lag.shape, F32), unroll=5)


def own_kernel(reach, taps_ref, modes_ref, tod_ref, basis_ref, fix_ref, own_ref, band):
    dishes, chans, tdev = tod_ref.shape
    groups = BLOCK // reach
    part = 64
    source = lax.broadcasted_iota(jnp.int32, (part, tdev), 0)
    target = lax.broadcasted_iota(jnp.int32, (part, tdev), 1)
    for start in range(0, tdev, part):
        pieces = split(taps_at(taps_ref, source + (start + reach) - target), 2)
        band[0, start:start + part] = pieces[0]
        band[1, start:start + part] = pieces[1]
    source = lax.broadcasted_iota(jnp.int32, (reach, tdev), 0)
    target = lax.broadcasted_iota(jnp.int32, (reach, tdev), 1)
    fix_ref[...] = jnp.zeros_like(fix_ref)
    for side, shift in ((0, 0), (1, tdev + reach)):
        pieces = split(taps_at(taps_ref, source + shift - target), 2)
        for group in range(groups):
            rows = pl.ds(side * BLOCK + group * reach, reach)
            fix_ref[0, group, rows, :] = pieces[0]
            fix_ref[1, group, rows, :] = pieces[1]
    basis_ref[...] = orth(modes_ref[...])
    size = 256

    def body(dish, carry):
        for start in range(0, chans, size):
            rows = pl.ds(start, size)
            series = tod_ref[dish, rows, :]
            high, low = split(series, 2)
            lowpass = mxu(high, band[0]) + (mxu(high, band[1]) + mxu(low, band[0]))
            own_ref[dish, rows, :] = series - lowpass
        return carry

    lax.fori_loop(0, dishes, body, 0)


def step(basis, high_ref, mid_ref):
    dishes, chans = high_ref.shape[0], high_ref.shape[1]
    left = rows_of(split(basis, 2))
    amounts = []
    for dish in range(dishes):
        product = folded(mxu(left, high_ref[dish]) + mxu(left, mid_ref[dish]), 2)
        amounts.append(rows_of(split(product, 2)))
    total = jnp.zeros((2 * ROWS, chans), F32)
    for dish in range(dishes):
        total = total + (
            mxu_last(amounts[dish], high_ref[dish]) + mxu_last(amounts[dish], mid_ref[dish])
        )
    return folded(total, 2)


def edge_kernel(basis_ref, fix_ref, own_ref, left_ref, right_ref, pointing_ref,
                high_ref, mid_ref, low_ref, total_ref):
    dishes, chans = own_ref.shape[0], own_ref.shape[1]
    groups = fix_ref.shape[1]
    size = chans // groups

    def body(dish, carry):
        edges = jnp.concatenate([left_ref[dish], right_ref[dish]], axis=1)
        high, low = split(edges, 2)
        for group in range(groups):
            rows = pl.ds(group * size, size)
            lowpass = mxu(high, fix_ref[0, group]) + (
                mxu(high, fix_ref[1, group]) + mxu(low, fix_ref[0, group])
            )
            pieces = split(own_ref[dish, rows, :] - lowpass, 3)
            high_ref[dish, rows, :] = pieces[0]
            mid_ref[dish, rows, :] = pieces[1]
            low_ref[dish, rows, :] = pieces[2]
        return carry

    lax.fori_loop(0, dishes, body, 0)
    total_ref[...] = step(basis_ref[...], high_ref, mid_ref)
    total_ref[MODES:MODES + 1] = pointing_ref[...]


def step_kernel(sums_ref, high_ref, mid_ref, total_ref):
    total_ref[...] = step(orth(sums_ref[...]), high_ref, mid_ref)


def clean_kernel(sums_ref, weight_ref, high_ref, mid_ref, low_ref, out_ref,
                 weighted_ref, sems, amounts_ref, spread_ref):
    dishes, chans, tdev = high_ref.shape
    basis = split(orth(sums_ref[...]), 3)
    left = rows_of(basis[:2])
    wide = [basis[i].astype(F32) for i in (0, 0, 0, 1, 1, 2)]
    spread_ref[...] = jnp.concatenate(wide, axis=0).T.astype(BF16)
    for dish in range(dishes):
        product = folded(mxu(left, high_ref[dish]) + mxu(left, mid_ref[dish]), 2)
        amounts = split(product, 3)
        amounts_ref[dish] = rows_of([amounts[i] for i in (0, 1, 2, 0, 1, 0)])
    per_dish = tdev // BLOCK
    owned = chans // (CHIPS * CORES)
    part = owned // CHIPS

    def copy_of(dish):
        blocks = pl.ds(dish * per_dish, per_dish)
        return pltpu.make_async_copy(
            weighted_ref.at[dish], out_ref.at[:, blocks], sems.at[dish]
        )

    def body(dish, carry):
        removed = mxu(spread_ref[...], amounts_ref[dish])
        weight = weight_ref[dish]
        for chip in range(CHIPS):
            for group in range(CHIPS * CORES):
                first = group * owned + chip * part
                rows = pl.ds(first, part)
                filtered = (low_ref[dish, rows, :].astype(F32)
                            + mid_ref[dish, rows, :].astype(F32)
                            ) + high_ref[dish, rows, :].astype(F32)
                weighted = (weight * (filtered - removed[first:first + part])).astype(BF16)
                for block in range(per_dish):
                    weighted_ref[dish, chip * CHIPS * CORES + group, block] = weighted[
                        :, block * BLOCK:(block + 1) * BLOCK
                    ]
        copy_of(dish).start()
        return carry

    lax.fori_loop(0, dishes, body, 0)
    for dish in range(dishes):
        copy_of(dish).wait()


def bin_kernel(pointing_ref, blocks_ref, sky_ref, *others):
    totals = (sky_ref,) + others
    for ref in totals:
        ref[...] = jnp.zeros_like(ref)
    sources, count, chans, width = blocks_ref.shape
    lane = lax.broadcasted_iota(jnp.int32, (chans, width), 1)

    def body(source, carry):
        for block in range(count):
            ref = totals[block % len(totals)]
            where = source * 2 * count + block
            tile = pointing_ref[where]
            offset = pointing_ref[where + count]
            half = offset >> (width.bit_length() - 1)
            shift = offset & (width - 1)
            moved = pltpu.roll(blocks_ref[source, block].astype(F32), shift, 1)
            first = jnp.where((lane >= shift) == (half == 0), moved, 0.0)
            ref[tile, :, 0:width] += first
            ref[tile, :, width:2 * width] += moved - first
        return carry

    lax.fori_loop(0, sources, body, 0)
    sky_ref[...] = (totals[0][...] + totals[1][...]) + (totals[2][...] + totals[3][...])


def call(kernel, name, out_shape, in_specs, scratch=(), out_specs=None):
    several = isinstance(out_shape, (list, tuple))
    if out_specs is None:
        out_specs = [VMEM] * len(out_shape) if several else VMEM
    return pl.pallas_call(
        kernel,
        out_shape=out_shape,
        in_specs=in_specs,
        out_specs=out_specs,
        scratch_shapes=scratch,
        compiler_params=PARAMS,
        name=name,
    )


def total_over(value, axes):
    for axis in axes:
        count = lax.axis_size(axis)
        parts = [value] + [
            lax.ppermute(value, axis, [(i, (i + s) % count) for i in range(count)])
            for s in range(1, count)
        ]
        while len(parts) > 1:
            parts = [a + b for a, b in zip(parts[::2], parts[1::2])]
        value = parts[0]
    return value


def shards(tod, taps, modes_init, weights, block_tile, block_offset):
    dishes, chans, tdev = tod.shape
    reach = (taps.shape[0] - 1) // 2
    groups = BLOCK // reach
    size = chans // groups
    per_dish = tdev // BLOCK
    times = CHIPS * CHIPS
    sharers = CHIPS * CHIPS * CORES
    part = chans // sharers
    rows_f32 = jax.ShapeDtypeStruct((ROWS, chans), F32)
    edge_f32 = jax.ShapeDtypeStruct((dishes, size, BLOCK), F32)
    piece = pltpu.VMEM((dishes, chans, tdev), BF16)

    with jax.named_scope("edges"):
        head, tail = call(
            lambda *refs: pack_kernel(reach, *refs), "pack", [edge_f32] * 2, [VMEM]
        )(tod)
        ends = times - 1
        from_left = lax.ppermute(tail, ("z", "x"), [(i, i + 1) for i in range(ends)])
        from_right = lax.ppermute(head, ("z", "x"), [(i + 1, i) for i in range(ends)])

    with jax.named_scope("own"):
        modes = jnp.pad(modes_init, ((0, ROWS - MODES), (0, 0)))
        basis, fix, own = call(
            lambda *refs: own_kernel(reach, *refs), "own",
            [rows_f32, jax.ShapeDtypeStruct((2, groups, tdev, tdev), BF16),
             pltpu.VMEM((dishes, chans, tdev), F32)],
            [SMEM, VMEM, VMEM],
            [pltpu.VMEM((2, tdev, tdev), BF16)],
        )(taps, modes, tod)

    with jax.named_scope("pointing"):
        mine = jnp.concatenate([block_tile.reshape(-1), block_offset.reshape(-1)]).astype(F32)
        slot = jnp.arange(sharers, dtype=jnp.int32)[:, None] == lax.axis_index(("x", "y", "c"))
        pointing = jnp.where(slot, mine[None, :], 0.0).reshape(1, sharers * mine.shape[0])

    with jax.named_scope("filtered"):
        high, mid, low, sums = call(
            edge_kernel, "edge", [piece, piece, piece, rows_f32], [VMEM] * 6
        )(basis, fix, own, from_left, from_right, pointing)

    with jax.named_scope("iterations"):
        sums = total_over(sums, ("c", "y", "x"))
        pointing = sums[MODES].astype(jnp.int32)
        sums = total_over(sums, ("z",))
        for _ in range(ITERS - 1):
            sums = call(step_kernel, "step", rows_f32, [VMEM] * 3)(sums, high, mid)
            sums = total_over(sums, ("c", "y", "x", "z"))

    with jax.named_scope("cleaned"):
        blocks = call(
            clean_kernel, "clean",
            pltpu.HBM((sharers, dishes * per_dish, part, BLOCK), BF16), [VMEM] * 5,
            [pltpu.VMEM((dishes, sharers, per_dish, part, BLOCK), BF16),
             pltpu.SemaphoreType.DMA((dishes,)),
             pltpu.VMEM((dishes, 6 * ROWS, tdev), BF16), pltpu.VMEM((chans, 6 * ROWS), BF16)],
            pl.BlockSpec(memory_space=pl.ANY),
        )(sums, weights.reshape(dishes, 1, tdev), high, mid, low)

    with jax.named_scope("channels"):
        arrived = lax.all_to_all(blocks, ("x", "y", "c"), 0, 0, tiled=True)

    with jax.named_scope("binning"):
        sky = call(
            bin_kernel, "bin", jax.ShapeDtypeStruct((times, part, PIX), F32), [SMEM, VMEM],
            [pltpu.VMEM((times, part, PIX), F32)] * 3,
        )(pointing, arrived)

    with jax.named_scope("tiles"):
        parts = lax.all_to_all(sky, ("z", "x"), 0, 0, tiled=True)
        parts = parts.reshape(CHIPS, CHIPS * part, PIX)
        return jnp.sum(parts, axis=0, keepdims=True)


def solution(mesh):
    chips = Mesh(mesh.devices.reshape(CHIPS, CHIPS, CHIPS, CORES), ("z", "x", "y", "c"))
    dish, time = ("y", "c"), ("z", "x")
    placed = (P(dish, None, time), P(), P(), P(dish, time), P(dish, time), P(dish, time))
    return jax.shard_map(
        shards, mesh=chips, in_specs=placed, out_specs=P(time, dish, None), check_vma=False
    )
```

```python
import jax
import jax.numpy as jnp
from jax import lax
from jax.experimental import pallas as pl
from jax.experimental.pallas import tpu as pltpu
from jax.sharding import Mesh
from jax.sharding import PartitionSpec as P

ITERS = 3
BLOCK = 128
PIX = 256
MODES = 6
ROWS = 8
CHIPS = 4
CORES = 2
F32 = jnp.float32
BF16 = jnp.bfloat16
PARAMS = pltpu.CompilerParams(vmem_limit_bytes=16 * 1024 * 1024)
VMEM = pl.BlockSpec(memory_space=pltpu.VMEM)
SMEM = pl.BlockSpec(memory_space=pltpu.SMEM)
HBM = pl.BlockSpec(memory_space=pltpu.HBM)
LAST = (((1,), (1,)), ((), ()))


def split(value, pieces):
    result = []
    for _ in range(pieces):
        piece = value.astype(BF16)
        result.append(piece)
        value = value - piece.astype(F32)
    return result


def rows_of(pieces):
    return jnp.concatenate([piece.astype(F32) for piece in pieces], axis=0).astype(BF16)


def folded(product, pieces):
    total = product[0:ROWS]
    for index in range(1, pieces):
        total = total + product[index * ROWS:(index + 1) * ROWS]
    return total


def mxu(left, right):
    return jnp.dot(left, right, preferred_element_type=F32)


def mxu_last(left, right):
    return lax.dot_general(left, right, LAST, preferred_element_type=F32)


def orth(rows):
    row = lax.broadcasted_iota(jnp.int32, (rows.shape[0], 1), 0)
    squares = jnp.ones((rows.shape[0], 1), F32)
    for index in range(MODES):
        vector = rows[index:index + 1]
        inner = jnp.sum(rows * vector, axis=1, keepdims=True)
        square = inner[index:index + 1]
        squares = jnp.where(row == index, square, squares)
        rows = rows - jnp.where(row > index, inner / square, 0.0) * vector
    return jnp.where(row < MODES, rows / jnp.sqrt(squares), 0.0)


def pack_kernel(reach, tod_ref, head_ref, tail_ref, series_ref, sems):
    groups = BLOCK // reach
    dishes, chans, tdev = tod_ref.shape
    size = chans // groups
    lane = lax.broadcasted_iota(jnp.int32, (size, BLOCK), 1) // reach

    def copy_of(dish):
        return pltpu.make_async_copy(tod_ref.at[dish], series_ref.at[dish], sems.at[dish])

    for dish in range(dishes):
        copy_of(dish).start()

    def body(dish, carry):
        copy_of(dish).wait()
        head = jnp.zeros((size, BLOCK), F32)
        tail = jnp.zeros((size, BLOCK), F32)
        for group in range(groups):
            rows = pl.ds(group * size, size)
            first = series_ref[dish, rows, 0:BLOCK]
            last = series_ref[dish, rows, tdev - BLOCK:tdev]
            if group:
                first = pltpu.roll(first, group * reach, 1)
            move = (group * reach + reach) % BLOCK
            if move:
                last = pltpu.roll(last, move, 1)
            head = jnp.where(lane == group, first, head)
            tail = jnp.where(lane == group, last, tail)
        head_ref[dish] = head
        tail_ref[dish] = tail
        return carry

    lax.fori_loop(0, dishes, body, 0)


def taps_at(taps_ref, lag):
    def body(index, band):
        return jnp.where(lag == index, taps_ref[index], band)

    return lax.fori_loop(0, taps_ref.shape[0], body, jnp.zeros(lag.shape, F32), unroll=5)


def own_kernel(reach, taps_ref, modes_ref, tod_ref, basis_ref, fix_ref, own_ref, band):
    dishes, chans, tdev = tod_ref.shape
    groups = BLOCK // reach
    part = 64
    source = lax.broadcasted_iota(jnp.int32, (part, tdev), 0)
    target = lax.broadcasted_iota(jnp.int32, (part, tdev), 1)
    for start in range(0, tdev, part):
        pieces = split(taps_at(taps_ref, source + (start + reach) - target), 2)
        band[0, start:start + part] = pieces[0]
        band[1, start:start + part] = pieces[1]
    source = lax.broadcasted_iota(jnp.int32, (reach, tdev), 0)
    target = lax.broadcasted_iota(jnp.int32, (reach, tdev), 1)
    fix_ref[...] = jnp.zeros_like(fix_ref)
    for side, shift in ((0, 0), (1, tdev + reach)):
        pieces = split(taps_at(taps_ref, source + shift - target), 2)
        for group in range(groups):
            rows = pl.ds(side * BLOCK + group * reach, reach)
            fix_ref[0, group, rows, :] = pieces[0]
            fix_ref[1, group, rows, :] = pieces[1]
    basis_ref[...] = orth(modes_ref[...])
    size = 256

    def body(dish, carry):
        for start in range(0, chans, size):
            rows = pl.ds(start, size)
            series = tod_ref[dish, rows, :]
            high, low = split(series, 2)
            lowpass = mxu(high, band[0]) + (mxu(high, band[1]) + mxu(low, band[0]))
            own_ref[dish, rows, :] = series - lowpass
        return carry

    lax.fori_loop(0, dishes, body, 0)


def step(basis, high_ref, mid_ref):
    dishes, chans = high_ref.shape[0], high_ref.shape[1]
    left = rows_of(split(basis, 2))
    amounts = []
    for dish in range(dishes):
        product = folded(mxu(left, high_ref[dish]) + mxu(left, mid_ref[dish]), 2)
        amounts.append(rows_of(split(product, 2)))
    total = jnp.zeros((2 * ROWS, chans), F32)
    for dish in range(dishes):
        total = total + (
            mxu_last(amounts[dish], high_ref[dish]) + mxu_last(amounts[dish], mid_ref[dish])
        )
    return folded(total, 2)


def edge_kernel(basis_ref, fix_ref, own_ref, left_ref, right_ref, pointing_ref,
                high_ref, mid_ref, low_ref, total_ref):
    dishes, chans, tdev = own_ref.shape
    groups = fix_ref.shape[1]
    size = chans // groups
    several = 4

    def body(index, carry):
        some = pl.ds(index * several, several)
        edges = jnp.concatenate([left_ref[some], right_ref[some]], axis=2)
        high, low = split(edges.reshape(several * size, tdev), 2)
        for group in range(groups):
            rows = pl.ds(group * size, size)
            lowpass = mxu(high, fix_ref[0, group]) + (
                mxu(high, fix_ref[1, group]) + mxu(low, fix_ref[0, group])
            )
            pieces = split(own_ref[some, rows, :] - lowpass.reshape(several, size, tdev), 3)
            high_ref[some, rows, :] = pieces[0]
            mid_ref[some, rows, :] = pieces[1]
            low_ref[some, rows, :] = pieces[2]
        return carry

    lax.fori_loop(0, dishes // several, body, 0)
    total_ref[...] = step(basis_ref[...], high_ref, mid_ref)
    total_ref[MODES:MODES + 1] = pointing_ref[...]


def step_kernel(sums_ref, high_ref, mid_ref, total_ref):
    total_ref[...] = step(orth(sums_ref[...]), high_ref, mid_ref)


def clean_kernel(sums_ref, weight_ref, high_ref, mid_ref, low_ref, out_ref,
                 weighted_ref, sems, amounts_ref, spread_ref):
    dishes, chans, tdev = high_ref.shape
    basis = split(orth(sums_ref[...]), 3)
    left = rows_of(basis[:2])
    wide = [basis[i].astype(F32) for i in (0, 0, 0, 1, 1, 2)]
    spread_ref[...] = jnp.concatenate(wide, axis=0).T.astype(BF16)
    for dish in range(dishes):
        product = folded(mxu(left, high_ref[dish]) + mxu(left, mid_ref[dish]), 2)
        amounts = split(product, 3)
        amounts_ref[dish] = rows_of([amounts[i] for i in (0, 1, 2, 0, 1, 0)])
    per_dish = tdev // BLOCK
    owned = chans // (CHIPS * CORES)
    part = owned // CHIPS

    def copy_of(dish):
        blocks = pl.ds(dish * per_dish, per_dish)
        return pltpu.make_async_copy(
            weighted_ref.at[dish], out_ref.at[:, blocks], sems.at[dish]
        )

    def body(dish, carry):
        removed = mxu(spread_ref[...], amounts_ref[dish])
        weight = weight_ref[dish]
        for chip in range(CHIPS):
            for group in range(CHIPS * CORES):
                first = group * owned + chip * part
                rows = pl.ds(first, part)
                filtered = (low_ref[dish, rows, :].astype(F32)
                            + mid_ref[dish, rows, :].astype(F32)
                            ) + high_ref[dish, rows, :].astype(F32)
                weighted = (weight * (filtered - removed[first:first + part])).astype(BF16)
                for block in range(per_dish):
                    weighted_ref[dish, chip * CHIPS * CORES + group, block] = weighted[
                        :, block * BLOCK:(block + 1) * BLOCK
                    ]
        copy_of(dish).start()
        return carry

    lax.fori_loop(0, dishes, body, 0)
    for dish in range(dishes):
        copy_of(dish).wait()


def bin_kernel(pointing_ref, arrived_ref, sky_ref, blocks_ref, sems, *others):
    sources, count, chans, width = arrived_ref.shape
    pieces = sems.shape[0]
    several = sources // pieces

    def copy_of(piece):
        some = pl.ds(piece * several, several)
        return pltpu.make_async_copy(arrived_ref.at[some], blocks_ref.at[some], sems.at[piece])

    for piece in range(pieces):
        copy_of(piece).start()
    totals = (sky_ref,) + others
    for ref in totals:
        ref[...] = jnp.zeros_like(ref)
    lane = lax.broadcasted_iota(jnp.int32, (chans, width), 1)

    def one(source, carry):
        for block in range(count):
            ref = totals[block % len(totals)]
            where = source * 2 * count + block
            tile = pointing_ref[where]
            offset = pointing_ref[where + count]
            half = offset >> (width.bit_length() - 1)
            shift = offset & (width - 1)
            moved = pltpu.roll(blocks_ref[source, block].astype(F32), shift, 1)
            first = jnp.where((lane >= shift) == (half == 0), moved, 0.0)
            ref[tile, :, 0:width] += first
            ref[tile, :, width:2 * width] += moved - first
        return carry

    def body(piece, carry):
        copy_of(piece).wait()
        return lax.fori_loop(piece * several, (piece + 1) * several, one, carry)

    lax.fori_loop(0, pieces, body, 0)
    sky_ref[...] = (totals[0][...] + totals[1][...]) + (totals[2][...] + totals[3][...])


def call(kernel, name, out_shape, in_specs, scratch=(), out_specs=None):
    several = isinstance(out_shape, (list, tuple))
    if out_specs is None:
        out_specs = [VMEM] * len(out_shape) if several else VMEM
    return pl.pallas_call(
        kernel,
        out_shape=out_shape,
        in_specs=in_specs,
        out_specs=out_specs,
        scratch_shapes=scratch,
        compiler_params=PARAMS,
        name=name,
    )


def total_over(value, axes):
    for axis in axes:
        count = lax.axis_size(axis)
        parts = [value] + [
            lax.ppermute(value, axis, [(i, (i + s) % count) for i in range(count)])
            for s in range(1, count)
        ]
        while len(parts) > 1:
            parts = [a + b for a, b in zip(parts[::2], parts[1::2])]
        value = parts[0]
    return value


def shards(tod, taps, modes_init, weights, block_tile, block_offset):
    dishes, chans, tdev = tod.shape
    reach = (taps.shape[0] - 1) // 2
    groups = BLOCK // reach
    size = chans // groups
    per_dish = tdev // BLOCK
    times = CHIPS * CHIPS
    sharers = CHIPS * CHIPS * CORES
    part = chans // sharers
    rows_f32 = jax.ShapeDtypeStruct((ROWS, chans), F32)
    edge_f32 = jax.ShapeDtypeStruct((dishes, size, BLOCK), F32)
    piece = pltpu.VMEM((dishes, chans, tdev), BF16)

    with jax.named_scope("edges"):
        head, tail = call(
            lambda *refs: pack_kernel(reach, *refs), "pack", [edge_f32] * 2, [HBM],
            [pltpu.VMEM((dishes, chans, tdev), F32), pltpu.SemaphoreType.DMA((dishes,))],
        )(pltpu.with_memory_space_constraint(tod, pltpu.HBM))
        ends = times - 1
        from_left = lax.ppermute(tail, ("z", "x"), [(i, i + 1) for i in range(ends)])
        from_right = lax.ppermute(head, ("z", "x"), [(i + 1, i) for i in range(ends)])

    with jax.named_scope("own"):
        modes = jnp.pad(modes_init, ((0, ROWS - MODES), (0, 0)))
        basis, fix, own = call(
            lambda *refs: own_kernel(reach, *refs), "own",
            [rows_f32, jax.ShapeDtypeStruct((2, groups, tdev, tdev), BF16),
             pltpu.VMEM((dishes, chans, tdev), F32)],
            [SMEM, VMEM, VMEM],
            [pltpu.VMEM((2, tdev, tdev), BF16)],
        )(taps, modes, tod)

    with jax.named_scope("pointing"):
        mine = jnp.concatenate([block_tile.reshape(-1), block_offset.reshape(-1)]).astype(F32)
        slot = jnp.arange(sharers, dtype=jnp.int32)[:, None] == lax.axis_index(("x", "y", "c"))
        pointing = jnp.where(slot, mine[None, :], 0.0).reshape(1, sharers * mine.shape[0])

    with jax.named_scope("filtered"):
        high, mid, low, sums = call(
            edge_kernel, "edge", [piece, piece, piece, rows_f32], [VMEM] * 6
        )(basis, fix, own, from_left, from_right, pointing)

    with jax.named_scope("iterations"):
        sums = total_over(sums, ("c", "y", "x"))
        pointing = sums[MODES].astype(jnp.int32)
        sums = total_over(sums, ("z",))
        for _ in range(ITERS - 1):
            sums = call(step_kernel, "step", rows_f32, [VMEM] * 3)(sums, high, mid)
            sums = total_over(sums, ("c", "y", "x", "z"))

    with jax.named_scope("cleaned"):
        blocks = call(
            clean_kernel, "clean",
            pltpu.HBM((sharers, dishes * per_dish, part, BLOCK), BF16), [VMEM] * 5,
            [pltpu.VMEM((dishes, sharers, per_dish, part, BLOCK), BF16),
             pltpu.SemaphoreType.DMA((dishes,)),
             pltpu.VMEM((dishes, 6 * ROWS, tdev), BF16), pltpu.VMEM((chans, 6 * ROWS), BF16)],
            HBM,
        )(sums, weights.reshape(dishes, 1, tdev), high, mid, low)

    with jax.named_scope("channels"):
        arrived = lax.all_to_all(blocks, ("x", "y", "c"), 0, 0, tiled=True)

    with jax.named_scope("binning"):
        sky = call(
            bin_kernel, "bin", jax.ShapeDtypeStruct((times, part, PIX), F32), [SMEM, HBM],
            [pltpu.VMEM(blocks.shape, BF16), pltpu.SemaphoreType.DMA((8,))]
            + [pltpu.VMEM((times, part, PIX), F32)] * 3,
        )(pointing, arrived)

    with jax.named_scope("tiles"):
        parts = lax.all_to_all(sky, ("z", "x"), 0, 0, tiled=True)
        parts = parts.reshape(CHIPS, CHIPS * part, PIX)
        return jnp.sum(parts, axis=0, keepdims=True)


def solution(mesh):
    chips = Mesh(mesh.devices.reshape(CHIPS, CHIPS, CHIPS, CORES), ("z", "x", "y", "c"))
    dish, time = ("y", "c"), ("z", "x")
    placed = (P(dish, None, time), P(), P(), P(dish, time), P(dish, time), P(dish, time))
    return jax.shard_map(
        shards, mesh=chips, in_specs=placed, out_specs=P(time, dish, None), check_vma=False
    )
```

```python
import jax
import jax.numpy as jnp
from jax import lax
from jax.experimental import pallas as pl
from jax.experimental.pallas import tpu as pltpu
from jax.sharding import Mesh
from jax.sharding import PartitionSpec as P

ITERS = 3
BLOCK = 128
PIX = 256
MODES = 6
ROWS = 8
CHIPS = 4
CORES = 2
F32 = jnp.float32
BF16 = jnp.bfloat16
PARAMS = pltpu.CompilerParams(vmem_limit_bytes=14 * 1024 * 1024)
VMEM = pl.BlockSpec(memory_space=pltpu.VMEM)
SMEM = pl.BlockSpec(memory_space=pltpu.SMEM)
HBM = pl.BlockSpec(memory_space=pltpu.HBM)
LAST = (((1,), (1,)), ((), ()))


def split(value, pieces):
    result = []
    for _ in range(pieces):
        piece = value.astype(BF16)
        result.append(piece)
        value = value - piece.astype(F32)
    return result


def rows_of(pieces):
    return jnp.concatenate([piece.astype(F32) for piece in pieces], axis=0).astype(BF16)


def folded(product, pieces):
    total = product[0:ROWS]
    for index in range(1, pieces):
        total = total + product[index * ROWS:(index + 1) * ROWS]
    return total


def mxu(left, right):
    return jnp.dot(left, right, preferred_element_type=F32)


def mxu_last(left, right):
    return lax.dot_general(left, right, LAST, preferred_element_type=F32)


def orth(rows):
    row = lax.broadcasted_iota(jnp.int32, (rows.shape[0], 1), 0)
    squares = jnp.ones((rows.shape[0], 1), F32)
    for index in range(MODES):
        vector = rows[index:index + 1]
        inner = jnp.sum(rows * vector, axis=1, keepdims=True)
        square = inner[index:index + 1]
        squares = jnp.where(row == index, square, squares)
        rows = rows - jnp.where(row > index, inner / square, 0.0) * vector
    return jnp.where(row < MODES, rows / jnp.sqrt(squares), 0.0)


def pack_kernel(reach, tod_ref, head_ref, tail_ref, series_ref, sems):
    groups = BLOCK // reach
    dishes, chans, tdev = tod_ref.shape
    size = chans // groups
    lane = lax.broadcasted_iota(jnp.int32, (size, BLOCK), 1) // reach

    def copy_of(dish):
        return pltpu.make_async_copy(tod_ref.at[dish], series_ref.at[dish], sems.at[dish])

    for dish in range(dishes):
        copy_of(dish).start()

    def body(dish, carry):
        copy_of(dish).wait()
        head = jnp.zeros((size, BLOCK), F32)
        tail = jnp.zeros((size, BLOCK), F32)
        for group in range(groups):
            rows = pl.ds(group * size, size)
            first = series_ref[dish, rows, 0:BLOCK]
            last = series_ref[dish, rows, tdev - BLOCK:tdev]
            if group:
                first = pltpu.roll(first, group * reach, 1)
            move = (group * reach + reach) % BLOCK
            if move:
                last = pltpu.roll(last, move, 1)
            head = jnp.where(lane == group, first, head)
            tail = jnp.where(lane == group, last, tail)
        head_ref[dish] = head
        tail_ref[dish] = tail
        return carry

    lax.fori_loop(0, dishes, body, 0)


def taps_at(taps_ref, lag):
    def body(index, band):
        return jnp.where(lag == index, taps_ref[index], band)

    return lax.fori_loop(0, taps_ref.shape[0], body, jnp.zeros(lag.shape, F32), unroll=5)


def own_kernel(reach, taps_ref, modes_ref, tod_ref, basis_ref, fix_ref, own_ref, band):
    dishes, chans, tdev = tod_ref.shape
    groups = BLOCK // reach
    part = 64
    source = lax.broadcasted_iota(jnp.int32, (part, tdev), 0)
    target = lax.broadcasted_iota(jnp.int32, (part, tdev), 1)
    for start in range(0, tdev, part):
        pieces = split(taps_at(taps_ref, source + (start + reach) - target), 2)
        band[0, start:start + part] = pieces[0]
        band[1, start:start + part] = pieces[1]
    source = lax.broadcasted_iota(jnp.int32, (reach, tdev), 0)
    target = lax.broadcasted_iota(jnp.int32, (reach, tdev), 1)
    fix_ref[...] = jnp.zeros_like(fix_ref)
    for side, shift in ((0, 0), (1, tdev + reach)):
        pieces = split(taps_at(taps_ref, source + shift - target), 2)
        for group in range(groups):
            rows = pl.ds(side * BLOCK + group * reach, reach)
            fix_ref[0, group, rows, :] = pieces[0]
            fix_ref[1, group, rows, :] = pieces[1]
    basis_ref[...] = orth(modes_ref[...])
    size = 256

    def body(dish, carry):
        for start in range(0, chans, size):
            rows = pl.ds(start, size)
            series = tod_ref[dish, rows, :]
            high, low = split(series, 2)
            lowpass = mxu(high, band[0]) + (mxu(high, band[1]) + mxu(low, band[0]))
            own_ref[dish, rows, :] = series - lowpass
        return carry

    lax.fori_loop(0, dishes, body, 0)


def step(basis, high_ref, mid_ref):
    dishes, chans = high_ref.shape[0], high_ref.shape[1]
    left = rows_of(split(basis, 2))
    amounts = []
    for dish in range(dishes):
        product = folded(mxu(left, high_ref[dish]) + mxu(left, mid_ref[dish]), 2)
        amounts.append(rows_of(split(product, 2)))
    total = jnp.zeros((2 * ROWS, chans), F32)
    for dish in range(dishes):
        total = total + (
            mxu_last(amounts[dish], high_ref[dish]) + mxu_last(amounts[dish], mid_ref[dish])
        )
    return folded(total, 2)


def edge_kernel(basis_ref, fix_ref, own_ref, left_ref, right_ref, pointing_ref,
                high_ref, mid_ref, low_ref, total_ref):
    dishes, chans, tdev = own_ref.shape
    groups = fix_ref.shape[1]
    size = chans // groups
    several = 4

    def body(index, carry):
        some = pl.ds(index * several, several)
        edges = jnp.concatenate([left_ref[some], right_ref[some]], axis=2)
        high, low = split(edges.reshape(several * size, tdev), 2)
        for group in range(groups):
            rows = pl.ds(group * size, size)
            lowpass = mxu(high, fix_ref[0, group]) + (
                mxu(high, fix_ref[1, group]) + mxu(low, fix_ref[0, group])
            )
            pieces = split(own_ref[some, rows, :] - lowpass.reshape(several, size, tdev), 3)
            high_ref[some, rows, :] = pieces[0]
            mid_ref[some, rows, :] = pieces[1]
            low_ref[some, rows, :] = pieces[2]
        return carry

    lax.fori_loop(0, dishes // several, body, 0)
    total_ref[...] = step(basis_ref[...], high_ref, mid_ref)
    total_ref[MODES:MODES + 1] = pointing_ref[...]


def step_kernel(sums_ref, high_ref, mid_ref, note_ref, total_ref):
    total_ref[...] = step(orth(sums_ref[...]), high_ref, mid_ref)
    total_ref[MODES:MODES + 1] = note_ref[...]


def clean_kernel(place_ref, sums_ref, weight_ref, high_ref, mid_ref, low_ref, *refs):
    out_refs = refs[:1 + CHIPS]
    flat_ref, ring_ref, sems, amounts_ref, spread_ref, removed_ref = refs[1 + CHIPS:]
    dishes, chans, tdev = high_ref.shape
    basis = split(orth(sums_ref[...]), 3)
    left = rows_of(basis[:2])
    wide = [basis[i].astype(F32) for i in (0, 0, 0, 1, 1, 2)]
    spread_ref[...] = jnp.concatenate(wide, axis=0).T.astype(BF16)
    for dish in range(dishes):
        product = folded(mxu(left, high_ref[dish]) + mxu(left, mid_ref[dish]), 2)
        amounts = split(product, 3)
        amounts_ref[dish] = rows_of([amounts[i] for i in (0, 1, 2, 0, 1, 0)])
    per_dish = tdev // BLOCK
    groups = CHIPS * CORES
    owned = chans // groups
    half = owned // 2
    part = half // CHIPS
    z, core = place_ref[0], place_ref[3]

    def copies_of(dish):
        blocks = pl.ds(dish * per_dish, per_dish)
        sources = [flat_ref.at[dish]] + [ring_ref.at[dish, s] for s in range(CHIPS)]
        return [
            pltpu.make_async_copy(source, out.at[:, blocks], sems.at[dish, index])
            for index, (source, out) in enumerate(zip(sources, out_refs))
        ]

    def body(dish, carry):
        removed_ref[...] = mxu(spread_ref[...], amounts_ref[dish])
        weight = weight_ref[dish]

        def weighted_of(first, length):
            rows = pl.ds(first, length)
            filtered = (low_ref[dish, rows, :].astype(F32) + mid_ref[dish, rows, :].astype(F32)
                        ) + high_ref[dish, rows, :].astype(F32)
            return (weight * (filtered - removed_ref[rows, :])).astype(BF16)

        for group in range(groups):
            weighted = weighted_of(group * owned, half)
            for chip in range(CHIPS):
                for block in range(per_dish):
                    flat_ref[dish, chip * groups + group, block] = weighted[
                        chip * part:(chip + 1) * part, block * BLOCK:(block + 1) * BLOCK
                    ]
        for shift in range(CHIPS):
            for other in range(CORES):
                inner = half + ((z + shift) & (CHIPS - 1)) * part
                for chip in range(CHIPS):
                    group = chip * CORES + (core + other) % CORES
                    weighted = weighted_of(pl.multiple_of(group * owned + inner, part), part)
                    for block in range(per_dish):
                        ring_ref[dish, shift, other, block, chip * part:(chip + 1) * part] = (
                            weighted[:, block * BLOCK:(block + 1) * BLOCK]
                        )
        for copy in copies_of(dish):
            copy.start()
        return carry

    lax.fori_loop(0, dishes, body, 0)
    for dish in range(dishes):
        for copy in copies_of(dish):
            copy.wait()


def add_block(ref, place, lane, offset, block):
    half = offset >> (BLOCK.bit_length() - 1)
    shift = offset & (BLOCK - 1)
    moved = pltpu.roll(block.astype(F32), shift, 1)
    first = jnp.where((lane >= shift) == (half == 0), moved, 0.0)
    ref[place, :, 0:BLOCK] += first
    ref[place, :, BLOCK:2 * BLOCK] += moved - first


def flat_bin_kernel(pointing_ref, arrived_ref, sky_ref, blocks_ref, sems, *others):
    sources, count, chans, width = arrived_ref.shape
    pieces = sems.shape[0]
    several = sources // pieces

    def copy_of(piece):
        some = pl.ds(piece * several, several)
        return pltpu.make_async_copy(arrived_ref.at[some], blocks_ref.at[some], sems.at[piece])

    for piece in range(pieces):
        copy_of(piece).start()
    totals = (sky_ref,) + others
    for ref in totals:
        ref[...] = jnp.zeros_like(ref)
    lane = lax.broadcasted_iota(jnp.int32, (chans, width), 1)

    def one(source, carry):
        for block in range(count):
            where = source * 2 * count + block
            add_block(totals[block % len(totals)], pointing_ref[where], lane,
                      pointing_ref[where + count], blocks_ref[source, block])
        return carry

    def body(piece, carry):
        copy_of(piece).wait()
        return lax.fori_loop(piece * several, (piece + 1) * several, one, carry)

    lax.fori_loop(0, pieces, body, 0)
    sky_ref[...] = (totals[0][...] + totals[1][...]) + (totals[2][...] + totals[3][...])


def ring_bin_kernel(place_ref, pointing_ref, *refs):
    near, far, outs, totals = (refs[i * CHIPS:(i + 1) * CHIPS] for i in range(4))
    count, chans, width = far[0].shape
    part = chans // CHIPS
    z, y, core = place_ref[0], place_ref[2], place_ref[3]
    for ref in totals:
        ref[...] = jnp.zeros_like(ref)
    lane = lax.broadcasted_iota(jnp.int32, (chans, width), 1)
    last = CHIPS - 1

    def body(block, carry):
        for shift in range(CHIPS):
            for other in range(CORES):
                source = ((z - shift) & last) * CORES + (core + other) % CORES
                where = source * 2 * count + block
                value = far[shift][block] if other else near[shift][0, block]
                add_block(totals[shift], pointing_ref[where], lane,
                          pointing_ref[where + count], value)
        return carry

    lax.fori_loop(0, count, body, 0)
    for shift in range(CHIPS):
        rows = pl.ds(pl.multiple_of(((y + shift) & last) * part, part), part)
        outs[shift][...] = (totals[0][:, rows, :] + totals[1][:, rows, :]) + (
            totals[2][:, rows, :] + totals[3][:, rows, :]
        )


def call(kernel, name, out_shape, in_specs, scratch=(), out_specs=None):
    several = isinstance(out_shape, (list, tuple))
    if out_specs is None:
        out_specs = [VMEM] * len(out_shape) if several else VMEM
    return pl.pallas_call(
        kernel,
        out_shape=out_shape,
        in_specs=in_specs,
        out_specs=out_specs,
        scratch_shapes=scratch,
        compiler_params=PARAMS,
        name=name,
    )


def total_over(value, axes):
    for axis in axes:
        count = lax.axis_size(axis)
        parts = [value] + [
            lax.ppermute(value, axis, [(i, (i + s) % count) for i in range(count)])
            for s in range(1, count)
        ]
        while len(parts) > 1:
            parts = [a + b for a, b in zip(parts[::2], parts[1::2])]
        value = parts[0]
    return value


def shards(tod, taps, modes_init, weights, block_tile, block_offset):
    dishes, chans, tdev = tod.shape
    reach = (taps.shape[0] - 1) // 2
    groups = BLOCK // reach
    size = chans // groups
    per_dish = tdev // BLOCK
    times = CHIPS * CHIPS
    sharers = CHIPS * CHIPS * CORES
    half = chans // (CHIPS * CORES) // 2
    part = half // CHIPS
    count = dishes * per_dish
    rows_f32 = jax.ShapeDtypeStruct((ROWS, chans), F32)
    edge_f32 = jax.ShapeDtypeStruct((dishes, size, BLOCK), F32)
    piece = pltpu.VMEM((dishes, chans, tdev), BF16)

    with jax.named_scope("edges"):
        head, tail = call(
            lambda *refs: pack_kernel(reach, *refs), "pack", [edge_f32] * 2, [HBM],
            [pltpu.VMEM((dishes, chans, tdev), F32), pltpu.SemaphoreType.DMA((dishes,))],
        )(pltpu.with_memory_space_constraint(tod, pltpu.HBM))
        ends = times - 1
        from_left = lax.ppermute(tail, ("z", "x"), [(i, i + 1) for i in range(ends)])
        from_right = lax.ppermute(head, ("z", "x"), [(i + 1, i) for i in range(ends)])

    with jax.named_scope("own"):
        modes = jnp.pad(modes_init, ((0, ROWS - MODES), (0, 0)))
        basis, fix, own = call(
            lambda *refs: own_kernel(reach, *refs), "own",
            [rows_f32, jax.ShapeDtypeStruct((2, groups, tdev, tdev), BF16),
             pltpu.VMEM((dishes, chans, tdev), F32)],
            [SMEM, VMEM, VMEM],
            [pltpu.VMEM((2, tdev, tdev), BF16)],
        )(taps, modes, tod)

    with jax.named_scope("pointing"):
        mine = jnp.concatenate([block_tile.reshape(-1), block_offset.reshape(-1)]).astype(F32)
        slots = jnp.arange(sharers, dtype=jnp.int32)[:, None]
        note, ring_note = [
            jnp.where(slots == lax.axis_index(axes), mine[None, :], 0.0).reshape(1, chans)
            for axes in (("x", "y", "c"), ("z", "c"))
        ]
        place = jnp.stack([lax.axis_index(axis) for axis in ("z", "x", "y", "c")])

    with jax.named_scope("filtered"):
        note, ring_note, no_note, place, own = lax.optimization_barrier(
            (note, ring_note, jnp.zeros_like(note), place, own)
        )
        high, mid, low, sums = call(
            edge_kernel, "edge", [piece, piece, piece, rows_f32], [VMEM] * 6
        )(basis, fix, own, from_left, from_right, note)

    with jax.named_scope("iterations"):
        sums = total_over(sums, ("c", "y", "x"))
        pointing = sums[MODES].astype(jnp.int32)
        sums = total_over(sums, ("z",))
        sums = call(step_kernel, "step", rows_f32, [VMEM] * 4)(sums, high, mid, ring_note)
        sums = total_over(sums, ("c", "z"))
        ring_pointing = sums[MODES].astype(jnp.int32)
        sums = total_over(sums, ("y", "x"))
        for _ in range(ITERS - 2):
            sums = call(step_kernel, "step", rows_f32, [VMEM] * 4)(
                sums, high, mid, no_note
            )
            sums = total_over(sums, ("c", "y", "x", "z"))

    with jax.named_scope("cleaned"):
        ring_shape = (CORES, count, half, BLOCK)
        flat, *ring = call(
            clean_kernel, "clean",
            [pltpu.HBM((sharers, count, part, BLOCK), BF16)]
            + [pltpu.HBM(ring_shape, BF16)] * CHIPS,
            [SMEM] + [VMEM] * 5,
            [pltpu.VMEM((dishes, sharers, per_dish, part, BLOCK), BF16),
             pltpu.VMEM((dishes, CHIPS, CORES, per_dish, half, BLOCK), BF16),
             pltpu.SemaphoreType.DMA((dishes, 1 + CHIPS)),
             pltpu.VMEM((dishes, 6 * ROWS, tdev), BF16), pltpu.VMEM((chans, 6 * ROWS), BF16),
             pltpu.VMEM((chans, tdev), F32)],
            [HBM] * (1 + CHIPS),
        )(place, sums, weights.reshape(dishes, 1, tdev), high, mid, low)

    def along(value, axis, shift):
        return lax.ppermute(value, axis, [(i, (i + shift) % CHIPS) for i in range(CHIPS)])

    with jax.named_scope("channels"):
        arrived = lax.all_to_all(flat, ("x", "y", "c"), 0, 0, tiled=True)
        near = [ring[0]] + [along(ring[s], "z", s) for s in range(1, CHIPS)]
        far = [lax.ppermute(value[1], "c", [(0, 1), (1, 0)]) for value in near]

    with jax.named_scope("binning"):
        row_sums = call(
            ring_bin_kernel, "ring_bin",
            [jax.ShapeDtypeStruct((times, part, PIX), F32)] * CHIPS,
            [SMEM, SMEM] + [VMEM] * (2 * CHIPS),
            [pltpu.VMEM((times, half, PIX), F32)] * 4,
        )(place, ring_pointing, *near, *far)
        sky = call(
            flat_bin_kernel, "flat_bin", jax.ShapeDtypeStruct((times, part, PIX), F32),
            [SMEM, HBM],
            [pltpu.VMEM(flat.shape, BF16), pltpu.SemaphoreType.DMA((8,))]
            + [pltpu.VMEM((times, part, PIX), F32)] * 3,
        )(pointing, arrived)

    with jax.named_scope("tiles"):
        last, sky = lax.optimization_barrier((row_sums[-1], sky))
        row_sums = [*row_sums[:-1], last]
        rows = [row_sums[0]] + [along(row_sums[s], "y", s) for s in range(1, CHIPS)]
        rows = (rows[0] + rows[1]) + (rows[2] + rows[3])
        parts = lax.all_to_all(
            jnp.concatenate([sky, rows], axis=1), ("z", "x"), 0, 0, tiled=True
        ).reshape(CHIPS, CHIPS, 2, part, PIX)
        flat_sky = jnp.sum(parts[:, :, 0], axis=0)
        ring_sky = jnp.sum(parts[:, :, 1], axis=1)
        return jnp.concatenate([flat_sky, ring_sky]).reshape(1, 2 * half, PIX)


def solution(mesh):
    chips = Mesh(mesh.devices.reshape(CHIPS, CHIPS, CHIPS, CORES), ("z", "x", "y", "c"))
    dish, time = ("y", "c"), ("z", "x")
    placed = (P(dish, None, time), P(), P(), P(dish, time), P(dish, time), P(dish, time))
    return jax.shard_map(
        shards, mesh=chips, in_specs=placed, out_specs=P(time, dish, None), check_vma=False
    )
```

```python
import jax
import jax.numpy as jnp
from jax import lax
from jax.experimental import pallas as pl
from jax.experimental.pallas import tpu as pltpu
from jax.sharding import Mesh
from jax.sharding import PartitionSpec as P

ITERS = 3
BLOCK = 128
PIX = 256
MODES = 6
ROWS = 8
CHIPS = 4
CORES = 2
F32 = jnp.float32
BF16 = jnp.bfloat16
PARAMS = pltpu.CompilerParams(vmem_limit_bytes=14 * 1024 * 1024)
VMEM = pl.BlockSpec(memory_space=pltpu.VMEM)
SMEM = pl.BlockSpec(memory_space=pltpu.SMEM)
HBM = pl.BlockSpec(memory_space=pltpu.HBM)
LAST = (((1,), (1,)), ((), ()))


def split(value, pieces):
    result = []
    for _ in range(pieces):
        piece = value.astype(BF16)
        result.append(piece)
        value = value - piece.astype(F32)
    return result


def rows_of(pieces):
    return jnp.concatenate([piece.astype(F32) for piece in pieces], axis=0).astype(BF16)


def folded(product, pieces):
    total = product[0:ROWS]
    for index in range(1, pieces):
        total = total + product[index * ROWS:(index + 1) * ROWS]
    return total


def mxu(left, right):
    return jnp.dot(left, right, preferred_element_type=F32)


def mxu_last(left, right):
    return lax.dot_general(left, right, LAST, preferred_element_type=F32)


def orth(rows):
    row = lax.broadcasted_iota(jnp.int32, (rows.shape[0], 1), 0)
    squares = jnp.ones((rows.shape[0], 1), F32)
    for index in range(MODES):
        vector = rows[index:index + 1]
        inner = jnp.sum(rows * vector, axis=1, keepdims=True)
        square = inner[index:index + 1]
        squares = jnp.where(row == index, square, squares)
        rows = rows - jnp.where(row > index, inner / square, 0.0) * vector
    return jnp.where(row < MODES, rows / jnp.sqrt(squares), 0.0)


def pack_kernel(reach, tod_ref, head_ref, tail_ref, series_ref, sems):
    groups = BLOCK // reach
    dishes, chans, tdev = tod_ref.shape
    size = chans // groups
    lane = lax.broadcasted_iota(jnp.int32, (size, BLOCK), 1) // reach

    def copy_of(dish):
        return pltpu.make_async_copy(tod_ref.at[dish], series_ref.at[dish], sems.at[dish])

    for dish in range(dishes):
        copy_of(dish).start()

    def body(dish, carry):
        copy_of(dish).wait()
        head = jnp.zeros((size, BLOCK), F32)
        tail = jnp.zeros((size, BLOCK), F32)
        for group in range(groups):
            rows = pl.ds(group * size, size)
            first = series_ref[dish, rows, 0:BLOCK]
            last = series_ref[dish, rows, tdev - BLOCK:tdev]
            if group:
                first = pltpu.roll(first, group * reach, 1)
            move = (group * reach + reach) % BLOCK
            if move:
                last = pltpu.roll(last, move, 1)
            head = jnp.where(lane == group, first, head)
            tail = jnp.where(lane == group, last, tail)
        head_ref[dish] = head
        tail_ref[dish] = tail
        return carry

    lax.fori_loop(0, dishes, body, 0)


def taps_at(taps_ref, lag):
    def body(index, band):
        return jnp.where(lag == index, taps_ref[index], band)

    return lax.fori_loop(0, taps_ref.shape[0], body, jnp.zeros(lag.shape, F32), unroll=5)


def own_kernel(reach, taps_ref, modes_ref, tod_ref, basis_ref, fix_ref, own_ref, band):
    dishes, chans, tdev = tod_ref.shape
    groups = BLOCK // reach
    part = 64
    source = lax.broadcasted_iota(jnp.int32, (part, tdev), 0)
    target = lax.broadcasted_iota(jnp.int32, (part, tdev), 1)
    for start in range(0, tdev, part):
        pieces = split(taps_at(taps_ref, source + (start + reach) - target), 2)
        band[0, start:start + part] = pieces[0]
        band[1, start:start + part] = pieces[1]
    source = lax.broadcasted_iota(jnp.int32, (reach, tdev), 0)
    target = lax.broadcasted_iota(jnp.int32, (reach, tdev), 1)
    fix_ref[...] = jnp.zeros_like(fix_ref)
    for side, shift in ((0, 0), (1, tdev + reach)):
        pieces = split(taps_at(taps_ref, source + shift - target), 2)
        for group in range(groups):
            rows = pl.ds(side * BLOCK + group * reach, reach)
            fix_ref[0, group, rows, :] = pieces[0]
            fix_ref[1, group, rows, :] = pieces[1]
    basis_ref[...] = orth(modes_ref[...])
    size = 256

    def body(dish, carry):
        for start in range(0, chans, size):
            rows = pl.ds(start, size)
            series = tod_ref[dish, rows, :]
            high, low = split(series, 2)
            lowpass = mxu(high, band[0]) + (mxu(high, band[1]) + mxu(low, band[0]))
            own_ref[dish, rows, :] = series - lowpass
        return carry

    lax.fori_loop(0, dishes, body, 0)


def step(basis, high_ref, mid_ref):
    dishes, chans = high_ref.shape[0], high_ref.shape[1]
    left = rows_of(split(basis, 2))
    amounts = []
    for dish in range(dishes):
        product = folded(mxu(left, high_ref[dish]) + mxu(left, mid_ref[dish]), 2)
        amounts.append(rows_of(split(product, 2)))
    total = jnp.zeros((2 * ROWS, chans), F32)
    for dish in range(dishes):
        total = total + (
            mxu_last(amounts[dish], high_ref[dish]) + mxu_last(amounts[dish], mid_ref[dish])
        )
    return folded(total, 2)


def edge_kernel(basis_ref, fix_ref, own_ref, left_ref, right_ref, pointing_ref,
                high_ref, mid_ref, low_ref, total_ref):
    dishes, chans, tdev = own_ref.shape
    groups = fix_ref.shape[1]
    size = chans // groups
    several = 4

    def body(index, carry):
        some = pl.ds(index * several, several)
        edges = jnp.concatenate([left_ref[some], right_ref[some]], axis=2)
        high, low = split(edges.reshape(several * size, tdev), 2)
        for group in range(groups):
            rows = pl.ds(group * size, size)
            lowpass = mxu(high, fix_ref[0, group]) + (
                mxu(high, fix_ref[1, group]) + mxu(low, fix_ref[0, group])
            )
            pieces = split(own_ref[some, rows, :] - lowpass.reshape(several, size, tdev), 3)
            high_ref[some, rows, :] = pieces[0]
            mid_ref[some, rows, :] = pieces[1]
            low_ref[some, rows, :] = pieces[2]
        return carry

    lax.fori_loop(0, dishes // several, body, 0)
    total_ref[...] = step(basis_ref[...], high_ref, mid_ref)
    total_ref[MODES:MODES + 1] = pointing_ref[...]


def step_kernel(sums_ref, high_ref, mid_ref, note_ref, total_ref):
    total_ref[...] = step(orth(sums_ref[...]), high_ref, mid_ref)
    total_ref[MODES:MODES + 1] = note_ref[...]


def clean_kernel(place_ref, sums_ref, weight_ref, high_ref, mid_ref, low_ref, *refs):
    out_refs = refs[:1 + CHIPS]
    flat_ref, ring_ref, sems, amounts_ref, spread_ref = refs[1 + CHIPS:]
    dishes, chans, tdev = high_ref.shape
    basis = split(orth(sums_ref[...]), 3)
    left = rows_of(basis[:2])
    wide = [basis[i].astype(F32) for i in (0, 0, 0, 1, 1, 2)]
    spread_ref[...] = jnp.concatenate(wide, axis=0).T.astype(BF16)
    for dish in range(dishes):
        product = folded(mxu(left, high_ref[dish]) + mxu(left, mid_ref[dish]), 2)
        amounts = split(product, 3)
        amounts_ref[dish] = rows_of([amounts[i] for i in (0, 1, 2, 0, 1, 0)])
    per_dish = tdev // BLOCK
    groups = CHIPS * CORES
    owned = chans // groups
    half = owned // 2
    part = half // CHIPS
    z, core = place_ref[0], place_ref[3]

    def copies_of(dish):
        blocks = pl.ds(dish * per_dish, per_dish)
        sources = [flat_ref.at[dish]] + [ring_ref.at[dish, s] for s in range(CHIPS)]
        return [
            pltpu.make_async_copy(source, out.at[:, blocks], sems.at[dish, index])
            for index, (source, out) in enumerate(zip(sources, out_refs))
        ]

    def body(dish, carry):
        removed = mxu(spread_ref[...], amounts_ref[dish])
        weight = weight_ref[dish]
        for group in range(groups):
            chip, other = group // CORES, (group + core) % CORES
            rows = pl.ds(group * owned, owned)
            filtered = (low_ref[dish, rows, :].astype(F32) + mid_ref[dish, rows, :].astype(F32)
                        ) + high_ref[dish, rows, :].astype(F32)
            removed_here = removed[group * owned:(group + 1) * owned]
            weighted = (weight * (filtered - removed_here)).astype(BF16)
            for place in range(CHIPS):
                shift = (place - z) & (CHIPS - 1)
                for block in range(per_dish):
                    lanes = slice(block * BLOCK, (block + 1) * BLOCK)
                    first = place * part
                    flat_ref[dish, place * groups + group, block] = weighted[
                        first:first + part, lanes
                    ]
                    first += half
                    ring_ref[dish, shift, other, block, chip * part:(chip + 1) * part] = (
                        weighted[first:first + part, lanes]
                    )
        for copy in copies_of(dish):
            copy.start()
        return carry

    lax.fori_loop(0, dishes, body, 0)
    for dish in range(dishes):
        for copy in copies_of(dish):
            copy.wait()


def add_block(ref, place, lane, offset, block):
    half = offset >> (BLOCK.bit_length() - 1)
    shift = offset & (BLOCK - 1)
    moved = pltpu.roll(block.astype(F32), shift, 1)
    first = jnp.where((lane >= shift) == (half == 0), moved, 0.0)
    ref[place, :, 0:BLOCK] += first
    ref[place, :, BLOCK:2 * BLOCK] += moved - first


def flat_bin_kernel(pointing_ref, arrived_ref, sky_ref, blocks_ref, sems, *others):
    sources, count, chans, width = arrived_ref.shape
    pieces = sems.shape[0]
    several = sources // pieces

    def copy_of(piece):
        some = pl.ds(piece * several, several)
        return pltpu.make_async_copy(arrived_ref.at[some], blocks_ref.at[some], sems.at[piece])

    for piece in range(pieces):
        copy_of(piece).start()
    totals = (sky_ref,) + others
    for ref in totals:
        ref[...] = jnp.zeros_like(ref)
    lane = lax.broadcasted_iota(jnp.int32, (chans, width), 1)

    def one(source, carry):
        for block in range(count):
            where = source * 2 * count + block
            add_block(totals[block % len(totals)], pointing_ref[where], lane,
                      pointing_ref[where + count], blocks_ref[source, block])
        return carry

    def body(piece, carry):
        copy_of(piece).wait()
        return lax.fori_loop(piece * several, (piece + 1) * several, one, carry)

    lax.fori_loop(0, pieces, body, 0)
    sky_ref[...] = (totals[0][...] + totals[1][...]) + (totals[2][...] + totals[3][...])


def ring_bin_kernel(place_ref, pointing_ref, *refs):
    near, far, outs, totals = (refs[i * CHIPS:(i + 1) * CHIPS] for i in range(4))
    rest, totals = totals[0], refs[3 * CHIPS + 1:]
    count, chans, width = far[0].shape
    part = chans // CHIPS
    z, y, core = place_ref[0], place_ref[2], place_ref[3]
    for ref in totals:
        ref[...] = jnp.zeros_like(ref)
    lane = lax.broadcasted_iota(jnp.int32, (chans, width), 1)
    last = CHIPS - 1

    def body(block, carry):
        for shift in range(CHIPS):
            for other in range(CORES):
                source = ((z - shift) & last) * CORES + (core + other) % CORES
                where = source * 2 * count + block
                value = far[shift][block] if other else near[shift][0, block]
                add_block(totals[shift], pointing_ref[where], lane,
                          pointing_ref[where + count], value)
        return carry

    lax.fori_loop(0, count, body, 0)
    for shift in range(CHIPS):
        rows = pl.ds(pl.multiple_of(((y + shift) & last) * part, part), part)
        total = (totals[0][:, rows, :] + totals[1][:, rows, :]) + (
            totals[2][:, rows, :] + totals[3][:, rows, :]
        )
        tiles = outs[shift].shape[0]
        outs[shift][...] = total[:tiles]
        if tiles < total.shape[0]:
            rest[...] = total[tiles:]


def call(kernel, name, out_shape, in_specs, scratch=(), out_specs=None):
    several = isinstance(out_shape, (list, tuple))
    if out_specs is None:
        out_specs = [VMEM] * len(out_shape) if several else VMEM
    return pl.pallas_call(
        kernel,
        out_shape=out_shape,
        in_specs=in_specs,
        out_specs=out_specs,
        scratch_shapes=scratch,
        compiler_params=PARAMS,
        name=name,
    )


def total_over(value, axes):
    for axis in axes:
        count = lax.axis_size(axis)
        parts = [value] + [
            lax.ppermute(value, axis, [(i, (i + s) % count) for i in range(count)])
            for s in range(1, count)
        ]
        while len(parts) > 1:
            parts = [a + b for a, b in zip(parts[::2], parts[1::2])]
        value = parts[0]
    return value


def shards(tod, taps, modes_init, weights, block_tile, block_offset):
    dishes, chans, tdev = tod.shape
    reach = (taps.shape[0] - 1) // 2
    groups = BLOCK // reach
    size = chans // groups
    per_dish = tdev // BLOCK
    times = CHIPS * CHIPS
    sharers = CHIPS * CHIPS * CORES
    half = chans // (CHIPS * CORES) // 2
    part = half // CHIPS
    count = dishes * per_dish
    rows_f32 = jax.ShapeDtypeStruct((ROWS, chans), F32)
    edge_f32 = jax.ShapeDtypeStruct((dishes, size, BLOCK), F32)
    piece = pltpu.VMEM((dishes, chans, tdev), BF16)

    with jax.named_scope("edges"):
        head, tail = call(
            lambda *refs: pack_kernel(reach, *refs), "pack", [edge_f32] * 2, [HBM],
            [pltpu.VMEM((dishes, chans, tdev), F32), pltpu.SemaphoreType.DMA((dishes,))],
        )(pltpu.with_memory_space_constraint(tod, pltpu.HBM))
        ends = times - 1
        from_left = lax.ppermute(tail, ("z", "x"), [(i, i + 1) for i in range(ends)])
        from_right = lax.ppermute(head, ("z", "x"), [(i + 1, i) for i in range(ends)])

    with jax.named_scope("own"):
        modes = jnp.pad(modes_init, ((0, ROWS - MODES), (0, 0)))
        basis, fix, own = call(
            lambda *refs: own_kernel(reach, *refs), "own",
            [rows_f32, jax.ShapeDtypeStruct((2, groups, tdev, tdev), BF16),
             pltpu.VMEM((dishes, chans, tdev), F32)],
            [SMEM, VMEM, VMEM],
            [pltpu.VMEM((2, tdev, tdev), BF16)],
        )(taps, modes, tod)

    with jax.named_scope("pointing"):
        mine = jnp.concatenate([block_tile.reshape(-1), block_offset.reshape(-1)]).astype(F32)
        slots = jnp.arange(sharers, dtype=jnp.int32)[:, None]
        note, ring_note = [
            jnp.where(slots == lax.axis_index(axes), mine[None, :], 0.0).reshape(1, chans)
            for axes in (("x", "y", "c"), ("z", "c"))
        ]
        place = jnp.stack([lax.axis_index(axis) for axis in ("z", "x", "y", "c")])

    with jax.named_scope("filtered"):
        note, ring_note, no_note, place, own = lax.optimization_barrier(
            (note, ring_note, jnp.zeros_like(note), place, own)
        )
        high, mid, low, sums = call(
            edge_kernel, "edge", [piece, piece, piece, rows_f32], [VMEM] * 6
        )(basis, fix, own, from_left, from_right, note)

    with jax.named_scope("iterations"):
        sums = total_over(sums, ("c", "y", "x"))
        pointing = sums[MODES].astype(jnp.int32)
        sums = total_over(sums, ("z",))
        sums = call(step_kernel, "step", rows_f32, [VMEM] * 4)(sums, high, mid, ring_note)
        sums = total_over(sums, ("c", "z"))
        ring_pointing = sums[MODES].astype(jnp.int32)
        sums = total_over(sums, ("y", "x"))
        for _ in range(ITERS - 2):
            sums = call(step_kernel, "step", rows_f32, [VMEM] * 4)(
                sums, high, mid, no_note
            )
            sums = total_over(sums, ("c", "y", "x", "z"))

    with jax.named_scope("cleaned"):
        ring_shape = (CORES, count, half, BLOCK)
        flat, *ring = call(
            clean_kernel, "clean",
            [pltpu.HBM((sharers, count, part, BLOCK), BF16)]
            + [pltpu.HBM(ring_shape, BF16)] * CHIPS,
            [SMEM] + [VMEM] * 5,
            [pltpu.VMEM((dishes, sharers, per_dish, part, BLOCK), BF16),
             pltpu.VMEM((dishes, CHIPS, CORES, per_dish, half, BLOCK), BF16),
             pltpu.SemaphoreType.DMA((dishes, 1 + CHIPS)),
             pltpu.VMEM((dishes, 6 * ROWS, tdev), BF16), pltpu.VMEM((chans, 6 * ROWS), BF16)],
            [HBM] * (1 + CHIPS),
        )(place, sums, weights.reshape(dishes, 1, tdev), high, mid, low)

    def along(value, axis, shift):
        return lax.ppermute(value, axis, [(i, (i + shift) % CHIPS) for i in range(CHIPS)])

    with jax.named_scope("channels"):
        arrived = lax.all_to_all(flat, ("x", "y", "c"), 0, 0, tiled=True)
        near = [ring[0]] + [along(ring[s], "z", s) for s in range(1, CHIPS)]
        far = [lax.ppermute(value[1], "c", [(0, 1), (1, 0)]) for value in near]

    with jax.named_scope("binning"):
        row_sums = call(
            ring_bin_kernel, "ring_bin",
            [jax.ShapeDtypeStruct((tiles, part, PIX), F32)
             for tiles in [times] * (CHIPS - 1) + [times - 1, 1]],
            [SMEM, SMEM] + [VMEM] * (2 * CHIPS),
            [pltpu.VMEM((times, half, PIX), F32)] * 4,
        )(place, ring_pointing, *near, *far)
        sky = call(
            flat_bin_kernel, "flat_bin", jax.ShapeDtypeStruct((times, part, PIX), F32),
            [SMEM, HBM],
            [pltpu.VMEM(flat.shape, BF16), pltpu.SemaphoreType.DMA((8,))]
            + [pltpu.VMEM((times, part, PIX), F32)] * 3,
        )(pointing, arrived)

    with jax.named_scope("tiles"):
        rest, sky = lax.optimization_barrier((row_sums[-1], sky))
        rows = [row_sums[0]] + [along(row_sums[s], "y", s) for s in range(1, CHIPS)]
        rows[-1] = jnp.concatenate([rows[-1], along(rest, "y", CHIPS - 1)])
        rows = (rows[0] + rows[1]) + (rows[2] + rows[3])
        parts = lax.all_to_all(
            jnp.concatenate([sky, rows], axis=1), ("z", "x"), 0, 0, tiled=True
        ).reshape(CHIPS, CHIPS, 2, part, PIX)
        flat_sky = jnp.sum(parts[:, :, 0], axis=0)
        ring_sky = jnp.sum(parts[:, :, 1], axis=1)
        return jnp.concatenate([flat_sky, ring_sky]).reshape(1, 2 * half, PIX)


def solution(mesh):
    chips = Mesh(mesh.devices.reshape(CHIPS, CHIPS, CHIPS, CORES), ("z", "x", "y", "c"))
    dish, time = ("y", "c"), ("z", "x")
    placed = (P(dish, None, time), P(), P(), P(dish, time), P(dish, time), P(dish, time))
    return jax.shard_map(
        shards, mesh=chips, in_specs=placed, out_specs=P(time, dish, None), check_vma=False
    )
```

```python
import jax
import jax.numpy as jnp
from jax import lax
from jax.experimental import pallas as pl
from jax.experimental.pallas import tpu as pltpu
from jax.sharding import Mesh
from jax.sharding import PartitionSpec as P

ITERS = 3
BLOCK = 128
PIX = 256
MODES = 6
ROWS = 8
CHIPS = 4
CORES = 2
F32 = jnp.float32
BF16 = jnp.bfloat16
PARAMS = pltpu.CompilerParams(vmem_limit_bytes=14 * 1024 * 1024)
VMEM = pl.BlockSpec(memory_space=pltpu.VMEM)
SMEM = pl.BlockSpec(memory_space=pltpu.SMEM)
HBM = pl.BlockSpec(memory_space=pltpu.HBM)
LAST = (((1,), (1,)), ((), ()))


def split(value, pieces):
    result = []
    for _ in range(pieces):
        piece = value.astype(BF16)
        result.append(piece)
        value = value - piece.astype(F32)
    return result


def rows_of(pieces):
    return jnp.concatenate([piece.astype(F32) for piece in pieces], axis=0).astype(BF16)


def folded(product, pieces):
    total = product[0:ROWS]
    for index in range(1, pieces):
        total = total + product[index * ROWS:(index + 1) * ROWS]
    return total


def mxu(left, right):
    return jnp.dot(left, right, preferred_element_type=F32)


def mxu_last(left, right):
    return lax.dot_general(left, right, LAST, preferred_element_type=F32)


def orth(rows):
    row = lax.broadcasted_iota(jnp.int32, (rows.shape[0], 1), 0)
    squares = jnp.ones((rows.shape[0], 1), F32)
    for index in range(MODES):
        vector = rows[index:index + 1]
        inner = jnp.sum(rows * vector, axis=1, keepdims=True)
        square = inner[index:index + 1]
        squares = jnp.where(row == index, square, squares)
        rows = rows - jnp.where(row > index, inner / square, 0.0) * vector
    return jnp.where(row < MODES, rows / jnp.sqrt(squares), 0.0)


def pack_kernel(reach, tod_ref, head_ref, tail_ref, series_ref, sems):
    groups = BLOCK // reach
    dishes, chans, tdev = tod_ref.shape
    size = chans // groups
    lane = lax.broadcasted_iota(jnp.int32, (size, BLOCK), 1) // reach

    def copy_of(dish):
        return pltpu.make_async_copy(tod_ref.at[dish], series_ref.at[dish], sems.at[dish])

    for dish in range(dishes):
        copy_of(dish).start()

    def body(dish, carry):
        copy_of(dish).wait()
        head = jnp.zeros((size, BLOCK), F32)
        tail = jnp.zeros((size, BLOCK), F32)
        for group in range(groups):
            rows = pl.ds(group * size, size)
            first = series_ref[dish, rows, 0:BLOCK]
            last = series_ref[dish, rows, tdev - BLOCK:tdev]
            if group:
                first = pltpu.roll(first, group * reach, 1)
            move = (group * reach + reach) % BLOCK
            if move:
                last = pltpu.roll(last, move, 1)
            head = jnp.where(lane == group, first, head)
            tail = jnp.where(lane == group, last, tail)
        head_ref[dish] = head
        tail_ref[dish] = tail
        return carry

    lax.fori_loop(0, dishes, body, 0)


def taps_at(taps_ref, lag):
    def body(index, band):
        return jnp.where(lag == index, taps_ref[index], band)

    return lax.fori_loop(0, taps_ref.shape[0], body, jnp.zeros(lag.shape, F32), unroll=5)


def own_kernel(reach, taps_ref, modes_ref, tod_ref, basis_ref, fix_ref, own_ref, band):
    dishes, chans, tdev = tod_ref.shape
    part = 64
    source = lax.broadcasted_iota(jnp.int32, (part, tdev), 0)
    target = lax.broadcasted_iota(jnp.int32, (part, tdev), 1)
    for start in range(0, tdev, part):
        pieces = split(taps_at(taps_ref, source + (start + reach) - target), 2)
        band[0, start:start + part] = pieces[0]
        band[1, start:start + part] = pieces[1]
    span = 2 * BLOCK
    target = lax.broadcasted_iota(jnp.int32, (part, span), 1)
    for start in range(0, span, part):
        source = lax.broadcasted_iota(jnp.int32, (part, span), 0) + start
        lag = jnp.where(source < BLOCK, 0, 2 * reach) + source % reach - target % reach
        lag = jnp.where(source // reach == target // reach, lag, -1)
        pieces = split(taps_at(taps_ref, lag), 2)
        fix_ref[0, start:start + part] = pieces[0]
        fix_ref[1, start:start + part] = pieces[1]
    basis_ref[...] = orth(modes_ref[...])
    size = 256

    def body(dish, carry):
        for start in range(0, chans, size):
            rows = pl.ds(start, size)
            series = tod_ref[dish, rows, :]
            high, low = split(series, 2)
            lowpass = mxu(high, band[0]) + (mxu(high, band[1]) + mxu(low, band[0]))
            own_ref[dish, rows, :] = series - lowpass
        return carry

    lax.fori_loop(0, dishes, body, 0)


def step(basis, high_ref, mid_ref):
    dishes, chans = high_ref.shape[0], high_ref.shape[1]
    left = rows_of(split(basis, 2))
    amounts = []
    for dish in range(dishes):
        product = folded(mxu(left, high_ref[dish]) + mxu(left, mid_ref[dish]), 2)
        amounts.append(rows_of(split(product, 2)))
    total = jnp.zeros((2 * ROWS, chans), F32)
    for dish in range(dishes):
        total = total + (
            mxu_last(amounts[dish], high_ref[dish]) + mxu_last(amounts[dish], mid_ref[dish])
        )
    return folded(total, 2)


def edge_kernel(reach, basis_ref, fix_ref, own_ref, left_ref, right_ref, pointing_ref,
                high_ref, mid_ref, low_ref, total_ref):
    dishes, chans, tdev = own_ref.shape
    groups = BLOCK // reach
    size = chans // groups
    several = 4
    lane = lax.broadcasted_iota(jnp.int32, (several * size, BLOCK), 1)

    def body(index, carry):
        some = pl.ds(index * several, several)
        edges = jnp.concatenate([left_ref[some], right_ref[some]], axis=2)
        high, low = split(edges.reshape(several * size, 2 * BLOCK), 2)
        lowpass = mxu(high, fix_ref[0]) + (mxu(high, fix_ref[1]) + mxu(low, fix_ref[0]))
        for group in range(groups):
            rows = pl.ds(group * size, size)
            for side in range(2):
                columns = slice(side * (tdev - BLOCK), side * (tdev - BLOCK) + BLOCK)
                term = lowpass[:, side * BLOCK:(side + 1) * BLOCK]
                move = (side * (BLOCK - reach) - group * reach) % BLOCK
                if move:
                    term = pltpu.roll(term, move, 1)
                edge = lane >= BLOCK - reach if side else lane < reach
                term = jnp.where(edge, term, 0.0).reshape(several, size, BLOCK)
                pieces = split(own_ref[some, rows, columns] - term, 3)
                high_ref[some, rows, columns] = pieces[0]
                mid_ref[some, rows, columns] = pieces[1]
                low_ref[some, rows, columns] = pieces[2]
        return carry

    lax.fori_loop(0, dishes // several, body, 0)
    total_ref[...] = step(basis_ref[...], high_ref, mid_ref)
    total_ref[MODES:MODES + 1] = pointing_ref[...]


def step_kernel(sums_ref, high_ref, mid_ref, note_ref, total_ref):
    total_ref[...] = step(orth(sums_ref[...]), high_ref, mid_ref)
    total_ref[MODES:MODES + 1] = note_ref[...]


def clean_kernel(place_ref, sums_ref, weight_ref, high_ref, mid_ref, low_ref, *refs):
    out_refs = refs[:1 + CHIPS]
    flat_ref, ring_ref, sems, amounts_ref, spread_ref = refs[1 + CHIPS:]
    dishes, chans, tdev = high_ref.shape
    basis = split(orth(sums_ref[...]), 3)
    left = rows_of(basis[:2])
    wide = [basis[i].astype(F32) for i in (0, 0, 0, 1, 1, 2)]
    spread_ref[...] = jnp.concatenate(wide, axis=0).T.astype(BF16)
    for dish in range(dishes):
        product = folded(mxu(left, high_ref[dish]) + mxu(left, mid_ref[dish]), 2)
        amounts = split(product, 3)
        amounts_ref[dish] = rows_of([amounts[i] for i in (0, 1, 2, 0, 1, 0)])
    per_dish = tdev // BLOCK
    groups = CHIPS * CORES
    owned = chans // groups
    half = owned // 2
    part = half // CHIPS
    z, core = place_ref[0], place_ref[3]

    def copies_of(dish):
        blocks = pl.ds(dish * per_dish, per_dish)
        sources = [flat_ref.at[dish]] + [ring_ref.at[dish, s] for s in range(CHIPS)]
        return [
            pltpu.make_async_copy(source, out.at[:, blocks], sems.at[dish, index])
            for index, (source, out) in enumerate(zip(sources, out_refs))
        ]

    def body(dish, carry):
        removed = mxu(spread_ref[...], amounts_ref[dish])
        weight = weight_ref[dish]
        for group in range(groups):
            chip, other = group // CORES, (group + core) % CORES
            rows = pl.ds(group * owned, owned)
            filtered = (low_ref[dish, rows, :].astype(F32) + mid_ref[dish, rows, :].astype(F32)
                        ) + high_ref[dish, rows, :].astype(F32)
            removed_here = removed[group * owned:(group + 1) * owned]
            weighted = (weight * (filtered - removed_here)).astype(BF16)
            for place in range(CHIPS):
                shift = (place - z) & (CHIPS - 1)
                for block in range(per_dish):
                    lanes = slice(block * BLOCK, (block + 1) * BLOCK)
                    first = place * part
                    flat_ref[dish, place * groups + group, block] = weighted[
                        first:first + part, lanes
                    ]
                    first += half
                    ring_ref[dish, shift, other, block, chip * part:(chip + 1) * part] = (
                        weighted[first:first + part, lanes]
                    )
        for copy in copies_of(dish):
            copy.start()
        return carry

    lax.fori_loop(0, dishes, body, 0)
    for dish in range(dishes):
        for copy in copies_of(dish):
            copy.wait()


def add_block(ref, place, lane, offset, block):
    half = offset >> (BLOCK.bit_length() - 1)
    shift = offset & (BLOCK - 1)
    moved = pltpu.roll(block.astype(F32), shift, 1)
    first = jnp.where((lane >= shift) == (half == 0), moved, 0.0)
    ref[place, :, 0:BLOCK] += first
    ref[place, :, BLOCK:2 * BLOCK] += moved - first


def flat_bin_kernel(pointing_ref, arrived_ref, sky_ref, blocks_ref, sems, *others):
    sources, count, chans, width = arrived_ref.shape
    pieces = sems.shape[0]
    several = sources // pieces

    def copy_of(piece):
        some = pl.ds(piece * several, several)
        return pltpu.make_async_copy(arrived_ref.at[some], blocks_ref.at[some], sems.at[piece])

    for piece in range(pieces):
        copy_of(piece).start()
    totals = (sky_ref,) + others
    for ref in totals:
        ref[...] = jnp.zeros_like(ref)
    lane = lax.broadcasted_iota(jnp.int32, (chans, width), 1)

    def one(source, carry):
        for block in range(count):
            where = source * 2 * count + block
            add_block(totals[block % len(totals)], pointing_ref[where], lane,
                      pointing_ref[where + count], blocks_ref[source, block])
        return carry

    def body(piece, carry):
        copy_of(piece).wait()
        return lax.fori_loop(piece * several, (piece + 1) * several, one, carry)

    lax.fori_loop(0, pieces, body, 0)
    sky_ref[...] = (totals[0][...] + totals[1][...]) + (totals[2][...] + totals[3][...])


def ring_bin_kernel(place_ref, pointing_ref, *refs):
    near, far, outs, totals = (refs[i * CHIPS:(i + 1) * CHIPS] for i in range(4))
    rest, totals = totals[0], refs[3 * CHIPS + 1:]
    count, chans, width = far[0].shape
    part = chans // CHIPS
    z, y, core = place_ref[0], place_ref[2], place_ref[3]
    for ref in totals:
        ref[...] = jnp.zeros_like(ref)
    lane = lax.broadcasted_iota(jnp.int32, (chans, width), 1)
    last = CHIPS - 1

    def body(block, carry):
        for shift in range(CHIPS):
            for other in range(CORES):
                source = ((z - shift) & last) * CORES + (core + other) % CORES
                where = source * 2 * count + block
                value = far[shift][block] if other else near[shift][0, block]
                add_block(totals[shift], pointing_ref[where], lane,
                          pointing_ref[where + count], value)
        return carry

    lax.fori_loop(0, count, body, 0)
    for shift in range(CHIPS):
        rows = pl.ds(pl.multiple_of(((y + shift) & last) * part, part), part)
        total = (totals[0][:, rows, :] + totals[1][:, rows, :]) + (
            totals[2][:, rows, :] + totals[3][:, rows, :]
        )
        tiles = outs[shift].shape[0]
        outs[shift][...] = total[:tiles]
        if tiles < total.shape[0]:
            rest[...] = total[tiles:]


def call(kernel, name, out_shape, in_specs, scratch=(), out_specs=None):
    several = isinstance(out_shape, (list, tuple))
    if out_specs is None:
        out_specs = [VMEM] * len(out_shape) if several else VMEM
    return pl.pallas_call(
        kernel,
        out_shape=out_shape,
        in_specs=in_specs,
        out_specs=out_specs,
        scratch_shapes=scratch,
        compiler_params=PARAMS,
        name=name,
    )


def total_over(value, axes):
    for axis in axes:
        count = lax.axis_size(axis)
        parts = [value] + [
            lax.ppermute(value, axis, [(i, (i + s) % count) for i in range(count)])
            for s in range(1, count)
        ]
        while len(parts) > 1:
            parts = [a + b for a, b in zip(parts[::2], parts[1::2])]
        value = parts[0]
    return value


def shards(tod, taps, modes_init, weights, block_tile, block_offset):
    dishes, chans, tdev = tod.shape
    reach = (taps.shape[0] - 1) // 2
    groups = BLOCK // reach
    size = chans // groups
    per_dish = tdev // BLOCK
    times = CHIPS * CHIPS
    sharers = CHIPS * CHIPS * CORES
    half = chans // (CHIPS * CORES) // 2
    part = half // CHIPS
    count = dishes * per_dish
    rows_f32 = jax.ShapeDtypeStruct((ROWS, chans), F32)
    edge_f32 = jax.ShapeDtypeStruct((dishes, size, BLOCK), F32)
    piece = pltpu.VMEM((dishes, chans, tdev), BF16)

    with jax.named_scope("edges"):
        head, tail = call(
            lambda *refs: pack_kernel(reach, *refs), "pack", [edge_f32] * 2, [HBM],
            [pltpu.VMEM((dishes, chans, tdev), F32), pltpu.SemaphoreType.DMA((dishes,))],
        )(pltpu.with_memory_space_constraint(tod, pltpu.HBM))
        ends = times - 1
        from_left = lax.ppermute(tail, ("z", "x"), [(i, i + 1) for i in range(ends)])
        from_right = lax.ppermute(head, ("z", "x"), [(i + 1, i) for i in range(ends)])

    with jax.named_scope("own"):
        modes = jnp.pad(modes_init, ((0, ROWS - MODES), (0, 0)))
        basis, fix, own = call(
            lambda *refs: own_kernel(reach, *refs), "own",
            [rows_f32, jax.ShapeDtypeStruct((2, 2 * BLOCK, 2 * BLOCK), BF16),
             pltpu.VMEM((dishes, chans, tdev), F32)],
            [SMEM, VMEM, VMEM],
            [pltpu.VMEM((2, tdev, tdev), BF16)],
        )(taps, modes, tod)

    with jax.named_scope("pointing"):
        mine = jnp.concatenate([block_tile.reshape(-1), block_offset.reshape(-1)]).astype(F32)
        slots = jnp.arange(sharers, dtype=jnp.int32)[:, None]
        note, ring_note = [
            jnp.where(slots == lax.axis_index(axes), mine[None, :], 0.0).reshape(1, chans)
            for axes in (("x", "y", "c"), ("z", "c"))
        ]
        place = jnp.stack([lax.axis_index(axis) for axis in ("z", "x", "y", "c")])

    with jax.named_scope("filtered"):
        note, ring_note, no_note, place, own = lax.optimization_barrier(
            (note, ring_note, jnp.zeros_like(note), place, own)
        )
        high, mid, low, sums = call(
            lambda *refs: edge_kernel(reach, *refs), "edge", [piece, piece, piece, rows_f32], [VMEM] * 6
        )(basis, fix, own, from_left, from_right, note)

    with jax.named_scope("iterations"):
        sums = total_over(sums, ("c", "y", "x"))
        pointing = sums[MODES].astype(jnp.int32)
        sums = total_over(sums, ("z",))
        sums = call(step_kernel, "step", rows_f32, [VMEM] * 4)(sums, high, mid, ring_note)
        sums = total_over(sums, ("c", "z"))
        ring_pointing = sums[MODES].astype(jnp.int32)
        sums = total_over(sums, ("y", "x"))
        for _ in range(ITERS - 2):
            sums = call(step_kernel, "step", rows_f32, [VMEM] * 4)(
                sums, high, mid, no_note
            )
            sums = total_over(sums, ("c", "y", "x", "z"))

    with jax.named_scope("cleaned"):
        ring_shape = (CORES, count, half, BLOCK)
        flat, *ring = call(
            clean_kernel, "clean",
            [pltpu.HBM((sharers, count, part, BLOCK), BF16)]
            + [pltpu.HBM(ring_shape, BF16)] * CHIPS,
            [SMEM] + [VMEM] * 5,
            [pltpu.VMEM((dishes, sharers, per_dish, part, BLOCK), BF16),
             pltpu.VMEM((dishes, CHIPS, CORES, per_dish, half, BLOCK), BF16),
             pltpu.SemaphoreType.DMA((dishes, 1 + CHIPS)),
             pltpu.VMEM((dishes, 6 * ROWS, tdev), BF16), pltpu.VMEM((chans, 6 * ROWS), BF16)],
            [HBM] * (1 + CHIPS),
        )(place, sums, weights.reshape(dishes, 1, tdev), high, mid, low)

    def along(value, axis, shift):
        return lax.ppermute(value, axis, [(i, (i + shift) % CHIPS) for i in range(CHIPS)])

    with jax.named_scope("channels"):
        arrived = lax.all_to_all(flat, ("x", "y", "c"), 0, 0, tiled=True)
        near = [ring[0]] + [along(ring[s], "z", s) for s in range(1, CHIPS)]
        far = [lax.ppermute(value[1], "c", [(0, 1), (1, 0)]) for value in near]

    with jax.named_scope("binning"):
        row_sums = call(
            ring_bin_kernel, "ring_bin",
            [jax.ShapeDtypeStruct((tiles, part, PIX), F32)
             for tiles in [times] * (CHIPS - 1) + [times - 1, 1]],
            [SMEM, SMEM] + [VMEM] * (2 * CHIPS),
            [pltpu.VMEM((times, half, PIX), F32)] * 4,
        )(place, ring_pointing, *near, *far)
        sky = call(
            flat_bin_kernel, "flat_bin", jax.ShapeDtypeStruct((times, part, PIX), F32),
            [SMEM, HBM],
            [pltpu.VMEM(flat.shape, BF16), pltpu.SemaphoreType.DMA((8,))]
            + [pltpu.VMEM((times, part, PIX), F32)] * 3,
        )(pointing, arrived)

    with jax.named_scope("tiles"):
        rest, sky = lax.optimization_barrier((row_sums[-1], sky))
        rows = [row_sums[0]] + [along(row_sums[s], "y", s) for s in range(1, CHIPS)]
        rows[-1] = jnp.concatenate([rows[-1], along(rest, "y", CHIPS - 1)])
        rows = (rows[0] + rows[1]) + (rows[2] + rows[3])
        parts = lax.all_to_all(
            jnp.concatenate([sky, rows], axis=1), ("z", "x"), 0, 0, tiled=True
        ).reshape(CHIPS, CHIPS, 2, part, PIX)
        flat_sky = jnp.sum(parts[:, :, 0], axis=0)
        ring_sky = jnp.sum(parts[:, :, 1], axis=1)
        return jnp.concatenate([flat_sky, ring_sky]).reshape(1, 2 * half, PIX)


def solution(mesh):
    chips = Mesh(mesh.devices.reshape(CHIPS, CHIPS, CHIPS, CORES), ("z", "x", "y", "c"))
    dish, time = ("y", "c"), ("z", "x")
    placed = (P(dish, None, time), P(), P(), P(dish, time), P(dish, time), P(dish, time))
    return jax.shard_map(
        shards, mesh=chips, in_specs=placed, out_specs=P(time, dish, None), check_vma=False
    )
```

```python
import jax
import jax.numpy as jnp
from jax import lax
from jax.experimental import pallas as pl
from jax.experimental.pallas import tpu as pltpu
from jax.sharding import Mesh
from jax.sharding import PartitionSpec as P

ITERS = 3
BLOCK = 128
PIX = 256
MODES = 6
ROWS = 8
CHIPS = 4
CORES = 2
F32 = jnp.float32
BF16 = jnp.bfloat16
PARAMS = pltpu.CompilerParams(vmem_limit_bytes=14 * 1024 * 1024)
VMEM = pl.BlockSpec(memory_space=pltpu.VMEM)
SMEM = pl.BlockSpec(memory_space=pltpu.SMEM)
HBM = pl.BlockSpec(memory_space=pltpu.HBM)
LAST = (((1,), (1,)), ((), ()))


def split(value, pieces):
    result = []
    for _ in range(pieces):
        piece = value.astype(BF16)
        result.append(piece)
        value = value - piece.astype(F32)
    return result


def rows_of(pieces):
    return jnp.concatenate([piece.astype(F32) for piece in pieces], axis=0).astype(BF16)


def folded(product, pieces):
    total = product[0:ROWS]
    for index in range(1, pieces):
        total = total + product[index * ROWS:(index + 1) * ROWS]
    return total


def mxu(left, right):
    return jnp.dot(left, right, preferred_element_type=F32)


def mxu_last(left, right):
    return lax.dot_general(left, right, LAST, preferred_element_type=F32)


def orth(rows):
    row = lax.broadcasted_iota(jnp.int32, (rows.shape[0], 1), 0)
    squares = jnp.ones((rows.shape[0], 1), F32)
    for index in range(MODES):
        vector = rows[index:index + 1]
        inner = jnp.sum(rows * vector, axis=1, keepdims=True)
        square = inner[index:index + 1]
        squares = jnp.where(row == index, square, squares)
        rows = rows - jnp.where(row > index, inner / square, 0.0) * vector
    return jnp.where(row < MODES, rows / jnp.sqrt(squares), 0.0)


def pack_kernel(reach, tod_ref, head_ref, tail_ref, series_ref, sems):
    groups = BLOCK // reach
    dishes, chans, tdev = tod_ref.shape
    size = chans // groups
    lane = lax.broadcasted_iota(jnp.int32, (size, BLOCK), 1) // reach

    def copy_of(dish):
        return pltpu.make_async_copy(tod_ref.at[dish], series_ref.at[dish], sems.at[dish])

    for dish in range(dishes):
        copy_of(dish).start()

    def body(dish, carry):
        copy_of(dish).wait()
        head = jnp.zeros((size, BLOCK), F32)
        tail = jnp.zeros((size, BLOCK), F32)
        for group in range(groups):
            rows = pl.ds(group * size, size)
            first = series_ref[dish, rows, 0:BLOCK]
            last = series_ref[dish, rows, tdev - BLOCK:tdev]
            if group:
                first = pltpu.roll(first, group * reach, 1)
            move = (group * reach + reach) % BLOCK
            if move:
                last = pltpu.roll(last, move, 1)
            head = jnp.where(lane == group, first, head)
            tail = jnp.where(lane == group, last, tail)
        head_ref[dish] = head
        tail_ref[dish] = tail
        return carry

    lax.fori_loop(0, dishes, body, 0)


def taps_at(taps_ref, lag):
    def body(index, band):
        return jnp.where(lag == index, taps_ref[index], band)

    return lax.fori_loop(0, taps_ref.shape[0], body, jnp.zeros(lag.shape, F32), unroll=5)


def own_kernel(reach, taps_ref, modes_ref, tod_ref, basis_ref, fix_ref, own_ref, band):
    dishes, chans, tdev = tod_ref.shape
    part = 64
    source = lax.broadcasted_iota(jnp.int32, (part, tdev), 0)
    target = lax.broadcasted_iota(jnp.int32, (part, tdev), 1)
    for start in range(0, tdev, part):
        pieces = split(taps_at(taps_ref, source + (start + reach) - target), 2)
        band[0, start:start + part] = pieces[0]
        band[1, start:start + part] = pieces[1]
    span = 2 * BLOCK
    target = lax.broadcasted_iota(jnp.int32, (part, span), 1)
    for start in range(0, span, part):
        source = lax.broadcasted_iota(jnp.int32, (part, span), 0) + start
        lag = jnp.where(source < BLOCK, 0, 2 * reach) + source % reach - target % reach
        lag = jnp.where(source // reach == target // reach, lag, -1)
        pieces = split(taps_at(taps_ref, lag), 2)
        fix_ref[0, start:start + part] = pieces[0]
        fix_ref[1, start:start + part] = pieces[1]
    basis_ref[...] = orth(modes_ref[...])
    size = 256

    def body(dish, carry):
        for start in range(0, chans, size):
            rows = pl.ds(start, size)
            series = tod_ref[dish, rows, :]
            high, low = split(series, 2)
            lowpass = mxu(high, band[0]) + (mxu(high, band[1]) + mxu(low, band[0]))
            own_ref[dish, rows, :] = series - lowpass
        return carry

    lax.fori_loop(0, dishes, body, 0)


def step(basis, high_ref, mid_ref):
    dishes, chans = high_ref.shape[0], high_ref.shape[1]
    left = rows_of(split(basis, 2))
    amounts = []
    for dish in range(dishes):
        product = folded(mxu(left, high_ref[dish]) + mxu(left, mid_ref[dish]), 2)
        amounts.append(rows_of(split(product, 2)))
    total = jnp.zeros((2 * ROWS, chans), F32)
    for dish in range(dishes):
        total = total + (
            mxu_last(amounts[dish], high_ref[dish]) + mxu_last(amounts[dish], mid_ref[dish])
        )
    return folded(total, 2)


def edge_kernel(reach, basis_ref, fix_ref, own_ref, left_ref, right_ref, pointing_ref,
                high_ref, mid_ref, low_ref, total_ref):
    dishes, chans, tdev = own_ref.shape
    groups = BLOCK // reach
    size = chans // groups
    several = 4
    lane = lax.broadcasted_iota(jnp.int32, (several * size, BLOCK), 1)

    def body(index, carry):
        some = pl.ds(index * several, several)
        edges = jnp.concatenate([left_ref[some], right_ref[some]], axis=2)
        high, low = split(edges.reshape(several * size, 2 * BLOCK), 2)
        lowpass = mxu(high, fix_ref[0]) + (mxu(high, fix_ref[1]) + mxu(low, fix_ref[0]))
        for group in range(groups):
            rows = pl.ds(group * size, size)
            for side in range(2):
                columns = slice(side * (tdev - BLOCK), side * (tdev - BLOCK) + BLOCK)
                term = lowpass[:, side * BLOCK:(side + 1) * BLOCK]
                move = (side * (BLOCK - reach) - group * reach) % BLOCK
                if move:
                    term = pltpu.roll(term, move, 1)
                edge = lane >= BLOCK - reach if side else lane < reach
                term = jnp.where(edge, term, 0.0).reshape(several, size, BLOCK)
                pieces = split(own_ref[some, rows, columns] - term, 3)
                high_ref[some, rows, columns] = pieces[0]
                mid_ref[some, rows, columns] = pieces[1]
                low_ref[some, rows, columns] = pieces[2]
        return carry

    lax.fori_loop(0, dishes // several, body, 0)
    total_ref[...] = step(basis_ref[...], high_ref, mid_ref)
    total_ref[MODES:MODES + 1] = pointing_ref[...]


def step_kernel(sums_ref, high_ref, mid_ref, note_ref, total_ref):
    total_ref[...] = step(orth(sums_ref[...]), high_ref, mid_ref)
    total_ref[MODES:MODES + 1] = note_ref[...]


def clean_kernel(place_ref, sums_ref, weight_ref, high_ref, mid_ref, low_ref, *refs):
    out_refs = refs[:1 + CHIPS]
    flat_ref, ring_ref, sems, amounts_ref, spread_ref = refs[1 + CHIPS:]
    dishes, chans, tdev = high_ref.shape
    basis = split(orth(sums_ref[...]), 3)
    left = rows_of(basis[:2])
    wide = [basis[i].astype(F32) for i in (0, 0, 0, 1, 1, 2)]
    spread_ref[...] = jnp.concatenate(wide, axis=0).T.astype(BF16)
    for dish in range(dishes):
        product = folded(mxu(left, high_ref[dish]) + mxu(left, mid_ref[dish]), 2)
        amounts = split(product, 3)
        amounts_ref[dish] = rows_of([amounts[i] for i in (0, 1, 2, 0, 1, 0)])
    per_dish = tdev // BLOCK
    groups = CHIPS * CORES
    owned = chans // groups
    half = owned // 2
    part = half // CHIPS
    z, core = place_ref[0], place_ref[3]

    def copies_of(dish):
        blocks = pl.ds(dish * per_dish, per_dish)
        sources = [flat_ref.at[dish]] + [ring_ref.at[dish, s] for s in range(CHIPS)]
        return [
            pltpu.make_async_copy(source, out.at[:, blocks], sems.at[dish, index])
            for index, (source, out) in enumerate(zip(sources, out_refs))
        ]

    def body(dish, carry):
        removed = mxu(spread_ref[...], amounts_ref[dish])
        weight = weight_ref[dish]
        for group in range(groups):
            chip, other = group // CORES, (group + core) % CORES
            rows = pl.ds(group * owned, owned)
            filtered = (low_ref[dish, rows, :].astype(F32) + mid_ref[dish, rows, :].astype(F32)
                        ) + high_ref[dish, rows, :].astype(F32)
            removed_here = removed[group * owned:(group + 1) * owned]
            weighted = (weight * (filtered - removed_here)).astype(BF16)
            for place in range(CHIPS):
                shift = (place - z) & (CHIPS - 1)
                for block in range(per_dish):
                    lanes = slice(block * BLOCK, (block + 1) * BLOCK)
                    first = place * part
                    flat_ref[dish, place * groups + group, block] = weighted[
                        first:first + part, lanes
                    ]
                    first += half
                    ring_ref[dish, shift, other, block, chip * part:(chip + 1) * part] = (
                        weighted[first:first + part, lanes]
                    )
        for copy in copies_of(dish):
            copy.start()
        return carry

    lax.fori_loop(0, dishes, body, 0)
    for dish in range(dishes):
        for copy in copies_of(dish):
            copy.wait()


def add_block(ref, place, lane, offset, block):
    half = offset >> (BLOCK.bit_length() - 1)
    shift = offset & (BLOCK - 1)
    moved = pltpu.roll(block.astype(F32), shift, 1)
    first = jnp.where((lane >= shift) == (half == 0), moved, 0.0)
    ref[place, :, 0:BLOCK] += first
    ref[place, :, BLOCK:2 * BLOCK] += moved - first


def flat_bin_kernel(pointing_ref, arrived_ref, sky_ref, blocks_ref, sems, *others):
    sources, count, chans, width = arrived_ref.shape
    pieces = sems.shape[0]
    several = sources // pieces

    def copy_of(piece):
        some = pl.ds(piece * several, several)
        return pltpu.make_async_copy(arrived_ref.at[some], blocks_ref.at[some], sems.at[piece])

    for piece in range(pieces):
        copy_of(piece).start()
    totals = (sky_ref,) + others
    for ref in totals:
        ref[...] = jnp.zeros_like(ref)
    lane = lax.broadcasted_iota(jnp.int32, (chans, width), 1)

    def one(source, carry):
        for block in range(count):
            where = source * 2 * count + block
            add_block(totals[block % len(totals)], pointing_ref[where], lane,
                      pointing_ref[where + count], blocks_ref[source, block])
        return carry

    def body(piece, carry):
        copy_of(piece).wait()
        return lax.fori_loop(piece * several, (piece + 1) * several, one, carry)

    lax.fori_loop(0, pieces, body, 0)
    sky_ref[...] = (totals[0][...] + totals[1][...]) + (totals[2][...] + totals[3][...])


def ring_bin_kernel(place_ref, pointing_ref, *refs):
    near, far, outs, totals = (refs[i * CHIPS:(i + 1) * CHIPS] for i in range(4))
    rest, totals = totals[0], refs[3 * CHIPS + 1:]
    count, chans, width = far[0].shape
    part = chans // CHIPS
    z, y, core = place_ref[0], place_ref[2], place_ref[3]
    for ref in totals:
        ref[...] = jnp.zeros_like(ref)
    lane = lax.broadcasted_iota(jnp.int32, (chans, width), 1)
    last = CHIPS - 1

    def body(block, carry):
        for shift in range(CHIPS):
            for other in range(CORES):
                source = ((z - shift) & last) * CORES + (core + other) % CORES
                where = source * 2 * count + block
                value = far[shift][block] if other else near[shift][0, block]
                add_block(totals[shift], pointing_ref[where], lane,
                          pointing_ref[where + count], value)
        return carry

    lax.fori_loop(0, count, body, 0)
    for shift in range(CHIPS):
        rows = pl.ds(pl.multiple_of(((y + shift) & last) * part, part), part)
        total = (totals[0][:, rows, :] + totals[1][:, rows, :]) + (
            totals[2][:, rows, :] + totals[3][:, rows, :]
        )
        tiles = outs[shift].shape[0]
        outs[shift][...] = total[:tiles]
        if tiles < total.shape[0]:
            rest[...] = total[tiles:]


def call(kernel, name, out_shape, in_specs, scratch=(), out_specs=None):
    several = isinstance(out_shape, (list, tuple))
    if out_specs is None:
        out_specs = [VMEM] * len(out_shape) if several else VMEM
    return pl.pallas_call(
        kernel,
        out_shape=out_shape,
        in_specs=in_specs,
        out_specs=out_specs,
        scratch_shapes=scratch,
        compiler_params=PARAMS,
        name=name,
    )


def total_over(value, axes):
    for axis in axes:
        count = lax.axis_size(axis)
        parts = [value] + [
            lax.ppermute(value, axis, [(i, (i + s) % count) for i in range(count)])
            for s in range(1, count)
        ]
        while len(parts) > 1:
            parts = [a + b for a, b in zip(parts[::2], parts[1::2])]
        value = parts[0]
    return value


def shards(tod, taps, modes_init, weights, block_tile, block_offset):
    dishes, chans, tdev = tod.shape
    reach = (taps.shape[0] - 1) // 2
    groups = BLOCK // reach
    size = chans // groups
    per_dish = tdev // BLOCK
    times = CHIPS * CHIPS
    sharers = CHIPS * CHIPS * CORES
    half = chans // (CHIPS * CORES) // 2
    part = half // CHIPS
    count = dishes * per_dish
    rows_f32 = jax.ShapeDtypeStruct((ROWS, chans), F32)
    edge_f32 = jax.ShapeDtypeStruct((dishes, size, BLOCK), F32)
    piece = pltpu.VMEM((dishes, chans, tdev), BF16)

    with jax.named_scope("edges"):
        head, tail = call(
            lambda *refs: pack_kernel(reach, *refs), "pack", [edge_f32] * 2, [HBM],
            [pltpu.VMEM((dishes, chans, tdev), F32), pltpu.SemaphoreType.DMA((dishes,))],
        )(pltpu.with_memory_space_constraint(tod, pltpu.HBM))
        ends = times - 1
        from_left = lax.ppermute(tail, ("z", "x"), [(i, i + 1) for i in range(ends)])
        from_right = lax.ppermute(head, ("z", "x"), [(i + 1, i) for i in range(ends)])

    with jax.named_scope("own"):
        modes = jnp.pad(modes_init, ((0, ROWS - MODES), (0, 0)))
        basis, fix, own = call(
            lambda *refs: own_kernel(reach, *refs), "own",
            [rows_f32, jax.ShapeDtypeStruct((2, 2 * BLOCK, 2 * BLOCK), BF16),
             pltpu.VMEM((dishes, chans, tdev), F32)],
            [SMEM, VMEM, VMEM],
            [pltpu.VMEM((2, tdev, tdev), BF16)],
        )(taps, modes, tod)

    with jax.named_scope("pointing"):
        mine = jnp.concatenate([block_tile.reshape(-1), block_offset.reshape(-1)]).astype(F32)
        slots = jnp.arange(sharers, dtype=jnp.int32)[:, None]
        note, ring_note = [
            jnp.where(slots == lax.axis_index(axes), mine[None, :], 0.0).reshape(1, chans)
            for axes in (("x", "y", "c"), ("z", "c"))
        ]
        place = jnp.stack([lax.axis_index(axis) for axis in ("z", "x", "y", "c")])

    with jax.named_scope("filtered"):
        note, ring_note, no_note, place, own = lax.optimization_barrier(
            (note, ring_note, jnp.zeros_like(note), place, own)
        )
        high, mid, low, sums = call(
            lambda *refs: edge_kernel(reach, *refs), "edge", [piece, piece, piece, rows_f32], [VMEM] * 6
        )(basis, fix, own, from_left, from_right, note)

    with jax.named_scope("iterations"):
        sums = total_over(sums, ("c", "y", "x"))
        pointing = sums[MODES].astype(jnp.int32)
        sums = total_over(sums, ("z",))
        sums = call(step_kernel, "step", rows_f32, [VMEM] * 4)(sums, high, mid, ring_note)
        sums = total_over(sums, ("c", "z"))
        ring_pointing = sums[MODES].astype(jnp.int32)
        sums = total_over(sums, ("y", "x"))
        for _ in range(ITERS - 2):
            sums = call(step_kernel, "step", rows_f32, [VMEM] * 4)(
                sums, high, mid, no_note
            )
            sums = total_over(sums, ("c", "y", "x", "z"))

    with jax.named_scope("cleaned"):
        ring_shape = (CORES, count, half, BLOCK)
        flat, *ring = call(
            clean_kernel, "clean",
            [pltpu.HBM((sharers, count, part, BLOCK), BF16)]
            + [pltpu.HBM(ring_shape, BF16)] * CHIPS,
            [SMEM] + [VMEM] * 5,
            [pltpu.VMEM((dishes, sharers, per_dish, part, BLOCK), BF16),
             pltpu.VMEM((dishes, CHIPS, CORES, per_dish, half, BLOCK), BF16),
             pltpu.SemaphoreType.DMA((dishes, 1 + CHIPS)),
             pltpu.VMEM((dishes, 6 * ROWS, tdev), BF16), pltpu.VMEM((chans, 6 * ROWS), BF16)],
            [HBM] * (1 + CHIPS),
        )(place, sums, weights.reshape(dishes, 1, tdev), high, mid, low)

    def along(value, axis, shift):
        return lax.ppermute(value, axis, [(i, (i + shift) % CHIPS) for i in range(CHIPS)])

    with jax.named_scope("channels"):
        arrived = lax.all_to_all(flat, ("x", "y", "c"), 0, 0, tiled=True)
        away = {s: along(ring[s], "z", s) for s in (2, 1, 3)}
        near = [ring[0]] + [away[s] for s in range(1, CHIPS)]
        far = [lax.ppermute(value[1], "c", [(0, 1), (1, 0)]) for value in near]

    with jax.named_scope("binning"):
        row_sums = call(
            ring_bin_kernel, "ring_bin",
            [jax.ShapeDtypeStruct((tiles, part, PIX), F32)
             for tiles in [times] * (CHIPS - 1) + [times - 1, 1]],
            [SMEM, SMEM] + [VMEM] * (2 * CHIPS),
            [pltpu.VMEM((times, half, PIX), F32)] * 4,
        )(place, ring_pointing, *near, *far)
        sky = call(
            flat_bin_kernel, "flat_bin", jax.ShapeDtypeStruct((times, part, PIX), F32),
            [SMEM, HBM],
            [pltpu.VMEM(flat.shape, BF16), pltpu.SemaphoreType.DMA((8,))]
            + [pltpu.VMEM((times, part, PIX), F32)] * 3,
        )(pointing, arrived)

    with jax.named_scope("tiles"):
        rest, sky = lax.optimization_barrier((row_sums[-1], sky))
        rows = [row_sums[0]] + [along(row_sums[s], "y", s) for s in range(1, CHIPS)]
        rows[-1] = jnp.concatenate([rows[-1], along(rest, "y", CHIPS - 1)])
        rows = (rows[0] + rows[1]) + (rows[2] + rows[3])
        parts = lax.all_to_all(
            jnp.concatenate([sky, rows], axis=1), ("z", "x"), 0, 0, tiled=True
        ).reshape(CHIPS, CHIPS, 2, part, PIX)
        flat_sky = jnp.sum(parts[:, :, 0], axis=0)
        ring_sky = jnp.sum(parts[:, :, 1], axis=1)
        return jnp.concatenate([flat_sky, ring_sky]).reshape(1, 2 * half, PIX)


def solution(mesh):
    chips = Mesh(mesh.devices.reshape(CHIPS, CHIPS, CHIPS, CORES), ("z", "x", "y", "c"))
    dish, time = ("y", "c"), ("z", "x")
    placed = (P(dish, None, time), P(), P(), P(dish, time), P(dish, time), P(dish, time))
    return jax.shard_map(
        shards, mesh=chips, in_specs=placed, out_specs=P(time, dish, None), check_vma=False
    )
```
